256 devices in a mesh: leaf: 256 (over y, x, z, core).
Axes of the slice: x: 4, y: 4, z: 8, core: 2. Of those that a mesh axis runs over, the one named last changes fastest.
Arguments:
- points: float32 [28, 524288], P(None, 'leaf'), may hold values from -3 to 3
- tree_order: int32 [256, 2048], P('leaf'), may hold values from 0 to 2047, each once within a row
- leaf_basis: bfloat16 [1024, 512, 256], P('leaf'), may hold values from -0.25 to 0.25
- local_transfer: bfloat16 [1792, 256, 256], P('leaf'), may hold values from -0.2651875 to 0.2651875
- local_coupling: bfloat16 [768, 256, 256], P('leaf'), may hold values from -0.375 to 0.375
- device_transfer: bfloat16 [256, 6, 256, 256], P('leaf'), may hold values from -0.2651875 to 0.2651875, as said below
- device_coupling: bfloat16 [256, 8, 256, 256], P('leaf'), may hold values from -5.091169 to 5.091169, as said below
- solution: float32 [524288, 128], P('leaf'), may hold values from -6 to 6
- residual: float32 [524288, 128], P('leaf'), may hold values from -40 to 40
- direction: float32 [524288, 128], P('leaf'), may hold values from -40 to 40
Outputs:
- new_solution: float32 [524288, 128], P('leaf')
- new_residual: float32 [524288, 128], P('leaf')
- new_direction: float32 [524288, 128], P('leaf')
The draws below stay inside these ranges and needn't reach their ends.
Inputs may be any that keep to these rules, and one draw needn't show every extreme that they name: `tree_order`: each row is a permutation of 0 to 2047. `device_transfer`: entry m - 1 of a device is the transfer matrix of its ancestor node that spans 2 ** m devices; every device under that node holds the same matrix. `device_coupling`: entry m of a device is the coupling matrix that multiplies the coefficients of the sibling of its ancestor spanning 2 ** m devices; the devices of the lower side hold B, those of the upper side its transpose.
All inputs are finite; a program needn't handle non-finite values.
Results may differ from the reference program's by a relative error of at most 0.035.
Values may be sent and summed in bfloat16 or wider, within the bound.
No kernel may reach another device: no remote copies, remote signals or barrier semaphores. Data moves between devices by JAX's collectives and lax.ppermute only.
A program may use at most 64 MiB of HBM per device.

```python
import jax
import jax.numpy as jnp
from jax import lax

LEAF_ROWS = 512
OFF_RANK = 256
COLUMNS = 128
FEATURES = 28
LEAVES_DEV = 4
ITERATIONS = 3
LOCAL_LEVELS = 2
DEVICE_LEVELS = 8
LEVELS = 10
ROWS_DEV = 2048
ALL_LEAVES = 1024
ALL_POINTS = 524288
N_LEAF = 256


def scaled_field(key, rise_log):
    key_own = jax.random.fold_in(key, 0)
    key_rows = jax.random.fold_in(key, 2)
    key_cols = jax.random.fold_in(key, 3)
    own_part = jax.random.normal(key_own, (ALL_POINTS, COLUMNS), jnp.float32)
    mixture = jnp.clip(own_part, -4.0, 4.0)
    devices_all = ALL_POINTS // ROWS_DEV
    position = (jnp.arange(ALL_POINTS, dtype=jnp.int32) // ROWS_DEV).astype(jnp.float32) / (devices_all - 1)
    row_log = rise_log * position + (1.0 - rise_log) * jax.random.uniform(key_rows, (ALL_POINTS,), jnp.float32)
    col_log = jax.random.uniform(key_cols, (COLUMNS,), jnp.float32)
    return mixture * (10.0 ** (row_log - 0.5))[:, None] * (10.0 ** (col_log - 0.5))[None, :]


def draw_residual(key, part):
    key = jax.random.fold_in(key, 21)
    return scaled_field(key, 0.4771)


def draw_direction(key, part):
    key = jax.random.fold_in(key, 22)
    return scaled_field(key, 0.4771)


def draw_local_transfer(key, part):
    key = jax.random.fold_in(key, 11)
    groups = ALL_LEAVES // LEAVES_DEV
    raw_draw = jax.random.normal(key, (groups * (2 * LEAVES_DEV - 1), OFF_RANK, OFF_RANK), jnp.float32)
    return (jnp.clip(raw_draw, -6.0, 6.0) * (0.7071 / OFF_RANK ** 0.5)).astype(jnp.bfloat16)


def draw_device_transfer(key, part):
    key = jax.random.fold_in(key, 12)
    groups = ALL_LEAVES // LEAVES_DEV
    raw_draw = jax.random.normal(key, (groups, DEVICE_LEVELS - 2, OFF_RANK, OFF_RANK), jnp.float32)
    raw_draw = jnp.clip(raw_draw, -6.0, 6.0) * (0.7071 / OFF_RANK ** 0.5)
    device_ids = jnp.arange(groups, dtype=jnp.int32)[:, None]
    heights = jnp.arange(1, DEVICE_LEVELS - 1, dtype=jnp.int32)[None, :]
    leaders = device_ids >> heights << heights
    return raw_draw[leaders, heights - 1].astype(jnp.bfloat16)


def draw_device_coupling(key, part):
    key = jax.random.fold_in(key, 13)
    groups = ALL_LEAVES // LEAVES_DEV
    raw_draw = jax.random.normal(key, (groups, DEVICE_LEVELS, OFF_RANK, OFF_RANK), jnp.float32)
    level_gain = 0.6 * 2.0 ** ((jnp.arange(DEVICE_LEVELS, dtype=jnp.float32) + LOCAL_LEVELS) * 0.5)
    raw_draw = jnp.clip(raw_draw, -6.0, 6.0) / OFF_RANK ** 0.5 * level_gain[None, :, None, None]
    device_ids = jnp.arange(groups, dtype=jnp.int32)[:, None]
    heights = jnp.arange(DEVICE_LEVELS, dtype=jnp.int32)[None, :]
    leaders = device_ids >> heights + 1 << heights + 1
    upper_side = device_ids >> heights & 1
    chosen = raw_draw[leaders, heights]
    flipped = jnp.swapaxes(chosen, -1, -2)
    return jnp.where((upper_side == 1)[:, :, None, None], flipped, chosen).astype(jnp.bfloat16)


def shard_levels(key, extent, cuts, least, top_value):
    level = 1.0
    for axis_at, parts in cuts:
        draws = jax.random.uniform(jax.random.fold_in(jax.random.fold_in(key, 6), axis_at), (parts,), jnp.float32, least / len(cuts), top_value / len(cuts))
        level = level * jnp.repeat(jnp.exp(draws), extent[axis_at] // parts).reshape((-1,) + (1,) * (len(extent) - 1 - axis_at))
    return level


def gaussian(stream_key, dims, scale, reach, shards=(), kind=jnp.bfloat16):
    entries = jax.random.normal(stream_key, dims, jnp.float32) * scale
    if len(shards) > 0:
        entries = shard_levels(stream_key, dims, shards, -0.22, 0.18) * entries
    return jnp.clip(entries, min=-reach, max=reach).astype(kind)


def setup_inputs(seed: int = 0) -> dict:
    key_of = jax.random.split(jax.random.key(seed), 11)
    return {
        "points": gaussian(key_of[0], (FEATURES, ALL_POINTS), 0.5, 3.0, ((1, 256),), jnp.float32),
        "tree_order": jax.vmap(lambda own: jax.random.permutation(own, ROWS_DEV))(jax.random.split(key_of[1], N_LEAF)).reshape((N_LEAF, ROWS_DEV)).astype(jnp.int32),
        "leaf_basis": gaussian(key_of[2], (ALL_LEAVES, LEAF_ROWS, OFF_RANK), LEAF_ROWS ** -0.5, 0.25, ((0, 256),)),
        "local_transfer": draw_local_transfer(jax.random.fold_in(key_of[10], 71), 0),
        "local_coupling": gaussian(key_of[4], (N_LEAF * (LEAVES_DEV - 1), OFF_RANK, OFF_RANK), OFF_RANK ** -0.5, 0.375, ((0, 256),)),
        "device_transfer": draw_device_transfer(jax.random.fold_in(key_of[10], 71), 0),
        "device_coupling": draw_device_coupling(jax.random.fold_in(key_of[10], 71), 0),
        "solution": gaussian(key_of[7], (ALL_POINTS, COLUMNS), 1.0, 6.0, ((0, 256),), jnp.float32),
        "residual": draw_residual(jax.random.fold_in(key_of[10], 71), 0),
        "direction": draw_direction(jax.random.fold_in(key_of[10], 71), 0),
    }


exact_mode = lax.Precision.HIGHEST
ridge_weight = 32.0
sharpness = 0.25


def leaf_kernel(leaf_points):
    squares = jnp.sum(leaf_points * leaf_points, axis=0)
    products = jnp.dot(leaf_points.T, leaf_points, precision=exact_mode, preferred_element_type=jnp.float32)
    return jnp.exp(-sharpness * (squares[:, None] + squares[None, :] - 2.0 * products)).astype(jnp.bfloat16)


def to_parent(coeffs, blocks):
    return jnp.einsum('nij,nic->njc', blocks.astype(jnp.float32), coeffs.astype(jnp.float32), precision=exact_mode)


def to_child(coeffs, blocks):
    return jnp.einsum('nij,njc->nic', blocks.astype(jnp.float32), coeffs.astype(jnp.float32), precision=exact_mode)


def reference(points, tree_order, leaf_basis, local_transfer, local_coupling, device_transfer, device_coupling, solution, residual, direction):
    offsets = (jnp.arange(N_LEAF, dtype=jnp.int32) * ROWS_DEV)[:, None]
    source = (tree_order.astype(jnp.int32) + offsets).reshape(-1)
    ordered = jnp.take(points, source, axis=1)
    tree_points = ordered.reshape(FEATURES, ALL_LEAVES, LEAF_ROWS).transpose(1, 0, 2)

    local_nodes = local_transfer.reshape(N_LEAF, 2 * LEAVES_DEV - 1, OFF_RANK, OFF_RANK)
    local_pairs = local_coupling.reshape(N_LEAF, LEAVES_DEV - 1, OFF_RANK, OFF_RANK)
    transfers = []
    couplings = []
    node_start = 0
    for height in range(LOCAL_LEVELS + 1):
        number = LEAVES_DEV >> height
        transfers.append(local_nodes[:, node_start:node_start + number].reshape(-1, OFF_RANK, OFF_RANK))
        node_start += number
    pair_start = 0
    for height in range(LOCAL_LEVELS):
        number = LEAVES_DEV >> (height + 1)
        couplings.append(local_pairs[:, pair_start:pair_start + number].reshape(-1, OFF_RANK, OFF_RANK))
        pair_start += number
    for height in range(1, DEVICE_LEVELS - 1):
        transfers.append(device_transfer[::2 ** height, height - 1])
    for height in range(DEVICE_LEVELS):
        couplings.append(device_coupling[::2 ** (height + 1), height])

    def apply_operator(low_dir, full_dir):
        pieces = low_dir.reshape(ALL_LEAVES, LEAF_ROWS, COLUMNS)

        def project(bundle):
            leaf_block, dir_block = bundle
            return jnp.dot(leaf_block.T, dir_block, preferred_element_type=jnp.float32).astype(jnp.bfloat16)

        upward = [lax.map(project, (leaf_basis, pieces))]
        for height in range(LEVELS - 1):
            term_block = to_parent(upward[height], transfers[height]).astype(jnp.bfloat16)
            upward.append((term_block[0::2].astype(jnp.float32) + term_block[1::2].astype(jnp.float32)).astype(jnp.bfloat16))
        sources = []
        for height in range(LEVELS):
            left_side = upward[height][0::2]
            right_side = upward[height][1::2]
            to_left = to_child(right_side, couplings[height]).astype(jnp.bfloat16)
            to_right = to_parent(left_side, couplings[height]).astype(jnp.bfloat16)
            sources.append(jnp.stack([to_left, to_right], axis=1).reshape(-1, OFF_RANK, COLUMNS))
        field_down = sources[LEVELS - 1]
        for height in range(LEVELS - 2, -1, -1):
            parent = jnp.repeat(field_down, 2, axis=0)
            field_down = (sources[height].astype(jnp.float32) + to_child(parent, transfers[height])).astype(jnp.bfloat16)

        def finish(bundle):
            leaf_spots, leaf_block, dir_block, coeff_block = bundle
            kernel = leaf_kernel(leaf_spots)
            near_part = jnp.dot(kernel, dir_block, preferred_element_type=jnp.float32)
            return near_part + jnp.dot(leaf_block, coeff_block, preferred_element_type=jnp.float32)

        applied = lax.map(finish, (tree_points, leaf_basis, pieces, field_down))
        return applied.reshape(ALL_POINTS, COLUMNS) + ridge_weight * full_dir

    norm_now = jnp.sum(residual * residual, axis=0)
    for step_index in range(ITERATIONS):
        applied = apply_operator(direction.astype(jnp.bfloat16), direction)
        step_size = norm_now / jnp.sum(direction * applied, axis=0)
        solution = solution + step_size * direction
        residual = residual - step_size * applied
        norm_next = jnp.sum(residual * residual, axis=0)
        direction = residual + (norm_next / norm_now) * direction
        norm_now = norm_next
    return solution, residual, direction
```

```python
import functools

import jax
import jax.numpy as jnp
from jax import lax
from jax.experimental import pallas as pl
from jax.experimental.pallas import tpu as pltpu
from jax.sharding import PartitionSpec as P

ITERATIONS = 3
ridge_weight = 32.0
sharpness = 0.25
LEAVES = 4
ROWS = 512
RANK = 256
COLS = 128
LEVELS = 8
PAYLOAD = RANK + 32
BF = jnp.bfloat16
F32 = jnp.float32


def dot(left, right):
    return jnp.dot(left, right, preferred_element_type=F32)


def params(size=48 << 20):
    return pltpu.CompilerParams(vmem_limit_bytes=size)


def whole(shape):
    return pl.BlockSpec(shape, lambda *_: (0,) * len(shape))


def partners(count):
    turn = {0: 6, 1: 7, 2: 4, 3: 5, 4: 2, 5: 3, 6: 0, 7: 1}
    levels = []
    for level in range(count.bit_length() - 1):
        pairs = []
        for i in range(count):
            if level == 3:
                j = i & ~14 | turn[i >> 1 & 7] << 1
            elif level in (5, 7):
                j = i ^ 3 << level - 1
            else:
                j = i ^ 1 << level
            pairs.append((i, j))
        levels.append(pairs)
    return levels


def split3(value):
    high = value.astype(BF)
    rest = value - high.astype(F32)
    mid = rest.astype(BF)
    low = (rest - mid.astype(F32)).astype(BF)
    return high, mid, low


def pack_sums(sums):
    high, mid, low = split3(sums)
    parts = [piece.astype(F32) for piece in (high, mid, low)] + [jnp.zeros((8, COLS), F32)]
    return jnp.concatenate(parts, axis=0).astype(BF)


def unpack_sums(packed):
    wide = packed.astype(F32)
    return wide[0:8] + wide[8:16] + wide[16:24]


def row_of(sums, index):
    return sums[index : index + 1]


def stack_rows(*rows):
    place = lax.broadcasted_iota(jnp.int32, (8, COLS), 0)
    total = jnp.zeros((8, COLS), F32)
    for index, row in enumerate(rows):
        total = total + jnp.where(place == index, row, 0.0)
    return total


def leaf_kernel(points_ref, order_ref, out_ref, pieces):
    @pl.when(pl.program_id(0) == 0)
    def _():
        value = points_ref[...]
        high, mid, low = split3(value)
        gap = jnp.zeros((4, value.shape[1]), F32)
        pieces[...] = jnp.concatenate(
            [high.astype(F32), gap, mid.astype(F32), gap, low.astype(F32), gap], axis=0
        ).astype(BF)

    total = pieces.shape[1]
    place = lax.broadcasted_iota(jnp.int32, (total, ROWS), 0)
    chosen = jnp.where(place == order_ref[0], 1.0, 0.0).astype(BF)
    moved = dot(pieces[...], chosen)
    high, mid, low = moved[0:32], moved[32:64], moved[64:96]
    full = high + mid + low
    half = -0.5 * jnp.sum(full * full, axis=0, keepdims=True)
    h3, m3, l3 = (piece.astype(F32) for piece in split3(half))
    one = jnp.ones_like(half)
    place8 = lax.broadcasted_iota(jnp.int32, (8, ROWS), 0)

    def rows8(*rows):
        block = jnp.zeros((8, ROWS), F32)
        for index, row in enumerate(rows):
            block = block + jnp.where(place8 == index, row, 0.0)
        return block

    pad = jnp.zeros((8, ROWS), F32)
    left = jnp.concatenate(
        [high, high, mid, high, low, mid, rows8(h3, m3, l3, one, one, one), pad], axis=0
    ).astype(BF)
    right = jnp.concatenate(
        [high, mid, high, low, high, mid, rows8(one, one, one, h3, m3, l3), pad], axis=0
    ).astype(BF)
    inner = lax.dot_general(
        left, right, (((0,), (0,)), ((), ())), preferred_element_type=F32
    )
    out_ref[0] = jnp.exp((2.0 * sharpness) * inner).astype(BF)


def make_kernels(points, order):
    features, total = points.shape
    return pl.pallas_call(
        leaf_kernel,
        grid=(LEAVES,),
        in_specs=[
            whole((features, total)),
            pl.BlockSpec((1, 1, ROWS), lambda i: (i, 0, 0)),
        ],
        out_specs=pl.BlockSpec((1, ROWS, ROWS), lambda i: (i, 0, 0)),
        out_shape=jax.ShapeDtypeStruct((LEAVES, ROWS, ROWS), BF),
        scratch_shapes=[pltpu.VMEM((96, total), BF)],
        compiler_params=params(),
        cost_estimate=pl.CostEstimate(
            flops=2 * LEAVES * (96 * total + 208 * ROWS) * ROWS,
            bytes_accessed=4 << 20,
            transcendentals=LEAVES * ROWS * ROWS,
        ),
        name="leaf_kernels",
    )(points, order.reshape(LEAVES, 1, ROWS))


def compose_kernel(basis, local_r, local_b, device_r, device_b, other_r, wide, tall, mix, up, down):
    first = [local_r[i] for i in range(LEAVES)]
    second = [local_r[LEAVES], local_r[LEAVES + 1]]
    for i in range(LEAVES):
        path = dot(first[i], second[i // 2]).astype(BF)
        reach = dot(basis[i], path).astype(BF)
        wide[i, :, :RANK] = reach
        wide[i, :, RANK:] = basis[i]
        tall[i, :RANK, :] = reach.T
        tall[i, RANK:, :] = basis[i].T
    flipped = [block.T for block in first]
    pair = local_b[2]
    across = [pair, pair.T]
    for i in range(LEAVES):
        side = dot(first[i], across[i // 2]).astype(BF)
        for j in range(LEAVES):
            if i == j:
                block = jnp.zeros((RANK, RANK), BF)
            elif i // 2 == j // 2:
                block = local_b[i // 2]
                if i % 2:
                    block = block.T
            else:
                block = dot(side, flipped[j]).astype(BF)
            mix[i * RANK : (i + 1) * RANK, j * RANK : (j + 1) * RANK] = block
    path = None
    for level in range(LEVELS):
        coupling = device_b[0, level]
        down[level, :RANK, :] = coupling
        if path is None:
            down[level, RANK:, :] = coupling
        else:
            down[level, RANK:, :] = dot(path, coupling).astype(BF)
        if level + 1 < LEVELS:
            step = local_r[LEAVES + 2] if level == 0 else device_r[0, level - 1]
            up[level, :, :RANK] = step.T
            up[level, :, RANK:] = other_r[level].T
            path = step if path is None else dot(path, step).astype(BF)


def compose(basis, local_r, local_b, device_r, device_b, other_r):
    shapes = [
        (LEAVES, ROWS, 2 * RANK),
        (LEAVES, 2 * RANK, ROWS),
        (LEAVES * RANK, LEAVES * RANK),
        (LEVELS - 1, RANK, 2 * RANK),
        (LEVELS, 2 * RANK, RANK),
    ]

    def entry(basis, local_r, local_b, device_r, device_b, *rest):
        others = [ref[...] for ref in rest[: LEVELS - 1]]
        compose_kernel(
            basis, local_r, local_b, device_r, device_b, others, *rest[LEVELS - 1 :]
        )

    operands = [basis, local_r, local_b, device_r, device_b] + list(other_r)
    return pl.pallas_call(
        entry,
        in_specs=[pl.BlockSpec(memory_space=pltpu.VMEM)] * len(operands),
        out_specs=[pl.BlockSpec(memory_space=pltpu.VMEM)] * len(shapes),
        out_shape=[jax.ShapeDtypeStruct(shape, BF) for shape in shapes],
        compiler_params=params(),
        name="compose",
    )(*operands)


def climb_kernel(own, got, up, down, *rest):
    if len(rest) == 3:
        field_in, out, field_out = rest
    else:
        out, field_out = rest
        field_in = None
    mine = own[:RANK]
    theirs = got[:RANK]
    moved = dot(up[0, :, :RANK], mine) + dot(up[0, :, RANK:], theirs)
    out[:RANK] = moved.astype(BF)
    felt = dot(down[0], theirs)
    energy = jnp.sum(mine.astype(F32) * felt[:RANK], axis=0, keepdims=True)
    zero = jnp.zeros_like(energy)
    sums = unpack_sums(own[RANK:]) + unpack_sums(got[RANK:])
    out[RANK:] = pack_sums(sums + stack_rows(zero, 2.0 * energy))
    if field_in is None:
        field_out[...] = felt[RANK:]
    else:
        field_out[...] = field_in[...] + felt[RANK:]


def climb(level, own, got, up, down, field):
    operands = [own, got, up, down] + ([] if field is None else [field])
    specs = [
        whole((PAYLOAD, COLS)),
        whole((PAYLOAD, COLS)),
        pl.BlockSpec((1, RANK, 2 * RANK), lambda i: (level, 0, 0)),
        pl.BlockSpec((1, 2 * RANK, RANK), lambda i: (level, 0, 0)),
    ] + ([] if field is None else [whole((RANK, COLS))])
    return pl.pallas_call(
        climb_kernel,
        grid=(1,),
        in_specs=specs,
        out_specs=[whole((PAYLOAD, COLS)), whole((RANK, COLS))],
        out_shape=[
            jax.ShapeDtypeStruct((PAYLOAD, COLS), BF),
            jax.ShapeDtypeStruct((RANK, COLS), F32),
        ],
        compiler_params=params(8 << 20),
        name="climb",
    )(*operands)


def finish_sweep(own, got, down, field_in, scalars_in, first, field, scalars):
    mine = own[:RANK]
    theirs = got[:RANK]
    felt = dot(down[0], theirs)
    field[...] = (field_in[...] + felt[RANK:]).astype(BF)
    energy = jnp.sum(mine.astype(F32) * felt[:RANK], axis=0, keepdims=True)
    sums = unpack_sums(own[RANK:]) + unpack_sums(got[RANK:])
    norm = row_of(sums, 0)
    curve = row_of(sums, 1) + 2.0 * energy
    if first:
        scalars[...] = stack_rows(norm, curve, norm / curve)
    else:
        turn = norm / scalars_in[0:1]
        bend = curve + turn * (2.0 * row_of(sums, 2) + turn * scalars_in[1:2])
        scalars[...] = stack_rows(norm, bend, norm / bend, turn)


def leaf_update(first, wide, base, near, residual, direction, image, solved, field, scalars):
    reach = wide[0]
    applied = base[...] + dot(reach[:, :RANK], field[...]) + dot(reach[:, RANK:], near[0])
    size = scalars[2:3]
    if first:
        step = direction[...]
        pushed = applied
    else:
        turn = scalars[3:4]
        step = residual[...] + turn * direction[...]
        pushed = applied + turn * image[...]
    return step, pushed, solved[...] + size * step, residual[...] - size * pushed


def leaf_apply(vector, kernel, tall, base, gathered, total, i):
    low = vector.astype(BF)
    out = dot(kernel[0], low) + ridge_weight * vector
    base[...] = out
    coeffs = dot(tall[0], low)
    gathered[i] = coeffs[RANK:].astype(BF)

    @pl.when(i == 0)
    def _():
        total[...] = coeffs[:RANK]

    @pl.when(i > 0)
    def _():
        total[...] += coeffs[:RANK]

    return out


def column_sum(value):
    return jnp.sum(value, axis=0, keepdims=True)


def add_sums(sums, i, rows):
    @pl.when(i == 0)
    def _():
        sums[...] = rows

    @pl.when(i > 0)
    def _():
        sums[...] += rows


def close_leaves(mix, gathered, total, sums, near, payload):
    packed = gathered[...].reshape(LEAVES * RANK, COLS)
    felt = dot(mix[...], packed)
    energy = column_sum(packed.astype(F32) * felt)
    near[...] = felt.astype(BF).reshape(LEAVES, RANK, COLS)
    payload[:RANK] = total[...].astype(BF)
    payload[RANK:] = pack_sums(sums[...] + stack_rows(jnp.zeros_like(energy), energy))


def begin_kernel(
    residual, direction, kernel, tall, mix, base, near, payload, gathered, total, sums
):
    i = pl.program_id(0)
    vector = direction[...]
    out = leaf_apply(vector, kernel, tall, base, gathered, total, i)
    here = residual[...]
    add_sums(sums, i, stack_rows(column_sum(here * here), column_sum(vector * out)))

    @pl.when(i == LEAVES - 1)
    def _():
        close_leaves(mix, gathered, total, sums, near, payload)


def turn_kernel(
    first,
    own,
    got,
    down,
    field_in,
    scalars_in,
    wide,
    base_in,
    near_in,
    residual,
    direction,
    image,
    solved,
    kernel,
    tall,
    mix,
    residual_out,
    direction_out,
    image_out,
    solved_out,
    base,
    near,
    payload,
    scalars,
    gathered,
    total,
    sums,
    field,
):
    i = pl.program_id(0)

    @pl.when(i == 0)
    def _():
        finish_sweep(own, got, down, field_in, scalars_in, first, field, scalars)

    step, pushed, solved_new, here = leaf_update(
        first, wide, base_in, near_in, residual, direction, image, solved, field, scalars
    )
    residual_out[...] = here
    direction_out[...] = step
    image_out[...] = pushed
    solved_out[...] = solved_new
    out = leaf_apply(here, kernel, tall, base, gathered, total, i)
    add_sums(
        sums,
        i,
        stack_rows(column_sum(here * here), column_sum(here * out), column_sum(here * pushed)),
    )

    @pl.when(i == LEAVES - 1)
    def _():
        close_leaves(mix, gathered, total, sums, near, payload)


def end_kernel(
    own,
    got,
    down,
    field_in,
    scalars_in,
    wide,
    base_in,
    near_in,
    residual,
    direction,
    image,
    solved,
    residual_out,
    direction_out,
    solved_out,
    scalars,
    sums,
    field,
):
    i = pl.program_id(0)

    @pl.when(i == 0)
    def _():
        finish_sweep(own, got, down, field_in, scalars_in, False, field, scalars)

    step, pushed, solved_new, here = leaf_update(
        False, wide, base_in, near_in, residual, direction, image, solved, field, scalars
    )
    residual_out[...] = here
    direction_out[...] = step
    solved_out[...] = solved_new
    add_sums(sums, i, stack_rows(column_sum(here * here)))


rows_spec = pl.BlockSpec((ROWS, COLS), lambda i: (i, 0))
kernel_spec = pl.BlockSpec((1, ROWS, ROWS), lambda i: (i, 0, 0))
wide_spec = pl.BlockSpec((1, ROWS, 2 * RANK), lambda i: (i, 0, 0))
tall_spec = pl.BlockSpec((1, 2 * RANK, ROWS), lambda i: (i, 0, 0))
mix_spec = whole((LEAVES * RANK, LEAVES * RANK))
near_spec = pl.BlockSpec((1, RANK, COLS), lambda i: (i, 0, 0))
near_whole = whole((LEAVES, RANK, COLS))
payload_spec = whole((PAYLOAD, COLS))
small_spec = whole((8, COLS))
field_spec = whole((RANK, COLS))
last_spec = pl.BlockSpec((1, 2 * RANK, RANK), lambda i: (LEVELS - 1, 0, 0))

vector_shape = jax.ShapeDtypeStruct((LEAVES * ROWS, COLS), F32)
near_shape = jax.ShapeDtypeStruct((LEAVES, RANK, COLS), BF)
payload_shape = jax.ShapeDtypeStruct((PAYLOAD, COLS), BF)
small_shape = jax.ShapeDtypeStruct((8, COLS), F32)


def leaf_scratch():
    return [
        pltpu.VMEM((LEAVES, RANK, COLS), BF),
        pltpu.VMEM((RANK, COLS), F32),
        pltpu.VMEM((8, COLS), F32),
    ]


def begin(residual, direction, kernels, tall, mix):
    return pl.pallas_call(
        begin_kernel,
        grid=(LEAVES,),
        in_specs=[rows_spec, rows_spec, kernel_spec, tall_spec, mix_spec],
        out_specs=[rows_spec, near_whole, payload_spec],
        out_shape=[vector_shape, near_shape, payload_shape],
        scratch_shapes=leaf_scratch(),
        compiler_params=params(),
        name="begin",
    )(residual, direction, kernels, tall, mix)


def turn(first, own, got, down, field, scalars, wide, base, near, vectors, kernels, tall, mix):
    return pl.pallas_call(
        functools.partial(turn_kernel, first),
        grid=(LEAVES,),
        in_specs=[
            payload_spec,
            payload_spec,
            last_spec,
            field_spec,
            small_spec,
            wide_spec,
            rows_spec,
            near_spec,
        ]
        + [rows_spec] * 4
        + [kernel_spec, tall_spec, mix_spec],
        out_specs=[rows_spec] * 5 + [near_whole, payload_spec, small_spec],
        out_shape=[vector_shape] * 5 + [near_shape, payload_shape, small_shape],
        scratch_shapes=leaf_scratch() + [pltpu.VMEM((RANK, COLS), BF)],
        compiler_params=params(),
        name="turn",
    )(own, got, down, field, scalars, wide, base, near, *vectors, kernels, tall, mix)


def end(own, got, down, field, scalars, wide, base, near, vectors):
    return pl.pallas_call(
        end_kernel,
        grid=(LEAVES,),
        in_specs=[
            payload_spec,
            payload_spec,
            last_spec,
            field_spec,
            small_spec,
            wide_spec,
            rows_spec,
            near_spec,
        ]
        + [rows_spec] * 4,
        out_specs=[rows_spec] * 3 + [small_spec, small_spec],
        out_shape=[vector_shape] * 3 + [small_shape, small_shape],
        scratch_shapes=[pltpu.VMEM((RANK, COLS), BF)],
        compiler_params=params(),
        name="end",
    )(own, got, down, field, scalars, wide, base, near, *vectors)


def per_device(
    count,
    points,
    tree_order,
    leaf_basis,
    local_transfer,
    local_coupling,
    device_transfer,
    device_coupling,
    solution,
    residual,
    direction,
):
    routes = partners(count)
    other = []
    for level in range(LEVELS - 1):
        matrix = local_transfer[6] if level == 0 else device_transfer[0, level - 1]
        other.append(lax.ppermute(matrix, "leaf", routes[level]))
    kernels = make_kernels(points, tree_order)
    wide, tall, mix, up, down = compose(
        leaf_basis, local_transfer, local_coupling, device_transfer, device_coupling, other
    )
    base, near, payload = begin(residual, direction, kernels, tall, mix)
    image = direction
    scalars = jnp.ones((8, COLS), F32)
    for step in range(ITERATIONS):
        field = None
        for level in range(LEVELS - 1):
            got = lax.ppermute(payload, "leaf", routes[level])
            payload, field = climb(level, payload, got, up, down, field)
        got = lax.ppermute(payload, "leaf", routes[LEVELS - 1])
        vectors = (residual, direction, image, solution)
        if step + 1 < ITERATIONS:
            residual, direction, image, solution, base, near, payload, scalars = turn(
                step == 0,
                payload,
                got,
                down,
                field,
                scalars,
                wide,
                base,
                near,
                vectors,
                kernels,
                tall,
                mix,
            )
        else:
            residual, direction, solution, scalars, sums = end(
                payload, got, down, field, scalars, wide, base, near, vectors
            )
    spread = jnp.broadcast_to(sums[0:1], (count, COLS))
    parts = lax.all_to_all(spread, "leaf", 0, 0, tiled=True)
    norm = jnp.sum(parts, axis=0, keepdims=True)
    direction = residual + norm / scalars[0:1] * direction
    return (solution, residual, direction)


def solution(mesh):
    placed = (
        P(None, "leaf"),
        P("leaf", None),
        P("leaf", None, None),
        P("leaf", None, None),
        P("leaf", None, None),
        P("leaf", None, None, None),
        P("leaf", None, None, None),
        P("leaf", None),
        P("leaf", None),
        P("leaf", None),
    )
    return jax.shard_map(
        functools.partial(per_device, mesh.shape["leaf"]),
        mesh=mesh,
        in_specs=placed,
        out_specs=(P("leaf", None), P("leaf", None), P("leaf", None)),
        check_vma=False,
    )
```

```python
import functools

import jax
import jax.numpy as jnp
from jax import lax
from jax.experimental import pallas as pl
from jax.experimental.pallas import tpu as pltpu
from jax.sharding import PartitionSpec as P

ITERATIONS = 3
ridge_weight = 32.0
sharpness = 0.25
LEAVES = 4
ROWS = 512
RANK = 256
COLS = 128
LEVELS = 8
PAYLOAD = RANK + 32
BF = jnp.bfloat16
F32 = jnp.float32


def dot(left, right):
    return jnp.dot(left, right, preferred_element_type=F32)


def params(size=16 << 20):
    return pltpu.CompilerParams(vmem_limit_bytes=size)


in_vmem = pl.BlockSpec(memory_space=pltpu.VMEM)


def whole(shape):
    return pl.BlockSpec(shape, lambda *_: (0,) * len(shape))


def partners(count):
    turn = {0: 6, 1: 7, 2: 4, 3: 5, 4: 2, 5: 3, 6: 0, 7: 1}
    levels = []
    for level in range(count.bit_length() - 1):
        pairs = []
        for i in range(count):
            if level == 3:
                j = i & ~14 | turn[i >> 1 & 7] << 1
            elif level in (5, 7):
                j = i ^ 3 << level - 1
            else:
                j = i ^ 1 << level
            pairs.append((i, j))
        levels.append(pairs)
    return levels


def split3(value):
    high = value.astype(BF)
    rest = value - high.astype(F32)
    mid = rest.astype(BF)
    low = (rest - mid.astype(F32)).astype(BF)
    return high, mid, low


def pack_sums(sums):
    high, mid, low = split3(sums)
    parts = [piece.astype(F32) for piece in (high, mid, low)] + [jnp.zeros((8, COLS), F32)]
    return jnp.concatenate(parts, axis=0).astype(BF)


def unpack_sums(packed):
    wide = packed.astype(F32)
    return wide[0:8] + wide[8:16] + wide[16:24]


def row_of(sums, index):
    return sums[index : index + 1]


def stack_rows(*rows):
    place = lax.broadcasted_iota(jnp.int32, (8, COLS), 0)
    total = jnp.zeros((8, COLS), F32)
    for index, row in enumerate(rows):
        total = total + jnp.where(place == index, row, 0.0)
    return total


def rows8(*rows):
    place = lax.broadcasted_iota(jnp.int32, (8, rows[0].shape[1]), 0)
    block = jnp.zeros(place.shape, F32)
    for index, row in enumerate(rows):
        block = block + jnp.where(place == index, row, 0.0)
    return block


def leaf_kernel(points_ref, order_ref, out_ref):
    value = points_ref[...]
    total = value.shape[1]
    gap = jnp.zeros((4, total), F32)
    pieces = []
    for piece in split3(value):
        pieces += [piece.astype(F32), gap]
    pieces = jnp.concatenate(pieces, axis=0).astype(BF)
    place = lax.broadcasted_iota(jnp.int32, (total, ROWS), 0)
    for i in range(LEAVES):
        picked = order_ref[:, i * ROWS : (i + 1) * ROWS]
        chosen = jnp.where(place == picked, 1.0, 0.0).astype(BF)
        moved = dot(pieces, chosen)
        high, mid, low = moved[0:32], moved[32:64], moved[64:96]
        full = high + mid + low
        half = -0.5 * jnp.sum(full * full, axis=0, keepdims=True)
        h3, m3, l3 = (piece.astype(F32) for piece in split3(half))
        one = jnp.ones_like(half)
        pad = jnp.zeros((8, ROWS), F32)
        left = jnp.concatenate(
            [high, high, mid, high, low, mid, rows8(h3, m3, l3, one, one, one), pad], axis=0
        ).astype(BF)
        right = jnp.concatenate(
            [high, mid, high, low, high, mid, rows8(one, one, one, h3, m3, l3), pad], axis=0
        ).astype(BF)
        inner = lax.dot_general(
            left, right, (((0,), (0,)), ((), ())), preferred_element_type=F32
        )
        out_ref[i] = jnp.exp((2.0 * sharpness) * inner).astype(BF)


def make_kernels(points, order):
    total = points.shape[1]
    return pl.pallas_call(
        leaf_kernel,
        in_specs=[in_vmem, in_vmem],
        out_specs=in_vmem,
        out_shape=jax.ShapeDtypeStruct((LEAVES, ROWS, ROWS), BF),
        compiler_params=params(),
        cost_estimate=pl.CostEstimate(
            flops=2 * LEAVES * (96 * total + 208 * ROWS) * ROWS,
            bytes_accessed=4 << 20,
            transcendentals=LEAVES * ROWS * ROWS,
        ),
        name="leaf_kernels",
    )(points, order)


def compose_kernel(basis, local_r, local_b, device_r, device_b, wide, tall, mix, down):
    first = [local_r[i] for i in range(LEAVES)]
    second = [local_r[LEAVES], local_r[LEAVES + 1]]
    for i in range(LEAVES):
        path = dot(first[i], second[i // 2]).astype(BF)
        reach = dot(basis[i], path).astype(BF)
        wide[i, :, :RANK] = reach
        wide[i, :, RANK:] = basis[i]
        tall[i, :RANK, :] = reach.T
        tall[i, RANK:, :] = basis[i].T
    flipped = [block.T for block in first]
    pair = local_b[2]
    across = [pair, pair.T]
    for i in range(LEAVES):
        side = dot(first[i], across[i // 2]).astype(BF)
        for j in range(LEAVES):
            if i == j:
                block = jnp.zeros((RANK, RANK), BF)
            elif i // 2 == j // 2:
                block = local_b[i // 2]
                if i % 2:
                    block = block.T
            else:
                block = dot(side, flipped[j]).astype(BF)
            mix[i * RANK : (i + 1) * RANK, j * RANK : (j + 1) * RANK] = block
    path = None
    for level in range(LEVELS):
        coupling = device_b[0, level]
        down[level, :RANK, :] = coupling
        if path is None:
            down[level, RANK:, :] = coupling
        else:
            down[level, RANK:, :] = dot(path, coupling).astype(BF)
        if level + 1 < LEVELS:
            step = local_r[LEAVES + 2] if level == 0 else device_r[0, level - 1]
            path = step if path is None else dot(path, step).astype(BF)


def compose(basis, local_r, local_b, device_r, device_b):
    shapes = [
        (LEAVES, ROWS, 2 * RANK),
        (LEAVES, 2 * RANK, ROWS),
        (LEAVES * RANK, LEAVES * RANK),
        (LEVELS, 2 * RANK, RANK),
    ]
    return pl.pallas_call(
        compose_kernel,
        in_specs=[in_vmem] * 5,
        out_specs=[in_vmem] * len(shapes),
        out_shape=[jax.ShapeDtypeStruct(shape, BF) for shape in shapes],
        compiler_params=params(),
        name="compose",
    )(basis, local_r, local_b, device_r, device_b)


def flip_kernel(local_r, device_r, *rest):
    out = rest[-1]
    for level in range(LEVELS - 1):
        step = local_r[LEAVES + 2] if level == 0 else device_r[0, level - 1]
        out[level, :, :RANK] = step.T
        out[level, :, RANK:] = rest[level][...].T


def flip(local_r, device_r, other_r):
    return pl.pallas_call(
        flip_kernel,
        in_specs=[in_vmem] * (2 + len(other_r)),
        out_specs=in_vmem,
        out_shape=jax.ShapeDtypeStruct((LEVELS - 1, RANK, 2 * RANK), BF),
        compiler_params=params(),
        name="flip",
    )(local_r, device_r, *other_r)


def climb_kernel(level, own, got, up, down, *rest):
    field_in = rest[0] if level else None
    out, field_out = rest[-2:]
    mine = own[:RANK]
    theirs = got[:RANK]
    moved = dot(up[level, :, :RANK], mine) + dot(up[level, :, RANK:], theirs)
    out[:RANK] = moved.astype(BF)
    felt = dot(down[level], theirs)
    energy = jnp.sum(mine.astype(F32) * felt[:RANK], axis=0, keepdims=True)
    zero = jnp.zeros_like(energy)
    sums = unpack_sums(own[RANK:]) + unpack_sums(got[RANK:])
    out[RANK:] = pack_sums(sums + stack_rows(zero, 2.0 * energy))
    if level:
        field_out[...] = field_in[...] + felt[RANK:]
    else:
        field_out[...] = felt[RANK:]


def climb(level, own, got, up, down, field):
    operands = [own, got, up, down] + ([field] if level else [])
    return pl.pallas_call(
        functools.partial(climb_kernel, level),
        in_specs=[in_vmem] * len(operands),
        out_specs=[in_vmem] * 2,
        out_shape=[payload_shape, field_shape],
        compiler_params=params(4 << 20),
        name="climb",
    )(*operands)


def finish_sweep(own, got, down, field_in, scalars_in, first):
    mine = own[:RANK]
    theirs = got[:RANK]
    felt = dot(down[LEVELS - 1], theirs)
    field = (field_in[...] + felt[RANK:]).astype(BF)
    energy = jnp.sum(mine.astype(F32) * felt[:RANK], axis=0, keepdims=True)
    sums = unpack_sums(own[RANK:]) + unpack_sums(got[RANK:])
    norm = row_of(sums, 0)
    curve = row_of(sums, 1) + 2.0 * energy
    if first:
        return field, norm, curve, norm / curve, None
    turn = norm / scalars_in[0:1]
    bend = curve + turn * (2.0 * row_of(sums, 2) + turn * scalars_in[1:2])
    return field, norm, bend, norm / bend, turn


def column_sum(value):
    return jnp.sum(value, axis=0, keepdims=True)


def leaf_apply(vector, kernel, tall):
    low = vector.astype(BF)
    coeffs = dot(tall, low)
    return dot(kernel, low) + ridge_weight * vector, coeffs[:RANK], coeffs[RANK:].astype(BF)


def close_leaves(mix, gathered, total, sums, near, payload):
    packed = jnp.concatenate(gathered, axis=0)
    felt = dot(mix[...], packed)
    energy = column_sum(packed.astype(F32) * felt)
    near[...] = felt.astype(BF).reshape(LEAVES, RANK, COLS)
    payload[:RANK] = total.astype(BF)
    payload[RANK:] = pack_sums(sums + stack_rows(jnp.zeros_like(energy), energy))


def begin_kernel(residual, direction, kernel, tall, mix, base, near, payload):
    total = sums = None
    gathered = []
    for i in range(LEAVES):
        rows = slice(i * ROWS, (i + 1) * ROWS)
        vector = direction[rows]
        out, coeffs, local = leaf_apply(vector, kernel[i], tall[i])
        base[rows] = out
        here = residual[rows]
        part = stack_rows(column_sum(here * here), column_sum(vector * out))
        total = coeffs if i == 0 else total + coeffs
        sums = part if i == 0 else sums + part
        gathered.append(local)
    close_leaves(mix, gathered, total, sums, near, payload)


def turn_kernel(first, own, got, down, field_in, scalars_in, wide, base_in, near_in, *rest):
    if first:
        residual, image, kernel, tall, mix = rest[:5]
        residual_out, image_out, base, near, payload, scalars = rest[5:]
    else:
        residual, direction, image, kernel, tall, mix = rest[:6]
        residual_out, direction_out, image_out, base, near, payload, scalars = rest[6:]
    field, norm, bend, size, beta = finish_sweep(own, got, down, field_in, scalars_in, first)
    scalars[...] = stack_rows(norm, bend, size)
    total = sums = None
    gathered = []
    for i in range(LEAVES):
        rows = slice(i * ROWS, (i + 1) * ROWS)
        pushed = base_in[rows] + dot(wide[i], jnp.concatenate([field, near_in[i]], axis=0))
        here = residual[rows]
        if not first:
            pushed = pushed + beta * image[rows]
            direction_out[rows] = here + beta * direction[rows]
        here = here - size * pushed
        residual_out[rows] = here
        image_out[rows] = pushed
        out, coeffs, local = leaf_apply(here, kernel[i], tall[i])
        base[rows] = out
        part = stack_rows(column_sum(here * here), column_sum(here * out), column_sum(here * pushed))
        total = coeffs if i == 0 else total + coeffs
        sums = part if i == 0 else sums + part
        gathered.append(local)
    close_leaves(mix, gathered, total, sums, near, payload)


def end_kernel(
    own,
    got,
    down,
    field_in,
    scalars_in,
    wide,
    base_in,
    near_in,
    residual,
    direction,
    image,
    residual_out,
    direction_out,
    scalars,
    sums_out,
):
    field, norm, bend, size, beta = finish_sweep(own, got, down, field_in, scalars_in, False)
    scalars[...] = stack_rows(norm, bend, size)
    sums = None
    for i in range(LEAVES):
        rows = slice(i * ROWS, (i + 1) * ROWS)
        pushed = base_in[rows] + dot(wide[i], jnp.concatenate([field, near_in[i]], axis=0))
        pushed = pushed + beta * image[rows]
        here = residual[rows]
        direction_out[rows] = here + beta * direction[rows]
        here = here - size * pushed
        residual_out[rows] = here
        part = column_sum(here * here)
        sums = part if i == 0 else sums + part
    sums_out[...] = jnp.broadcast_to(sums, sums_out.shape)


vector_shape = jax.ShapeDtypeStruct((LEAVES * ROWS, COLS), F32)
near_shape = jax.ShapeDtypeStruct((LEAVES, RANK, COLS), BF)
payload_shape = jax.ShapeDtypeStruct((PAYLOAD, COLS), BF)
field_shape = jax.ShapeDtypeStruct((RANK, COLS), F32)
small_shape = jax.ShapeDtypeStruct((8, COLS), F32)


def call(kernel, name, operands, shapes):
    return pl.pallas_call(
        kernel,
        in_specs=[in_vmem] * len(operands),
        out_specs=[in_vmem] * len(shapes),
        out_shape=shapes,
        compiler_params=params(),
        name=name,
    )(*operands)


def begin(residual, direction, kernels, tall, mix):
    return call(
        begin_kernel,
        "begin",
        (residual, direction, kernels, tall, mix),
        [vector_shape, near_shape, payload_shape],
    )


def turn(first, sweep, scalars, wide, base, near, residual, direction, image, kernels, tall, mix):
    vectors = (residual, image) if first else (residual, direction, image)
    results = call(
        functools.partial(turn_kernel, first),
        "turn",
        (*sweep, scalars, wide, base, near, *vectors, kernels, tall, mix),
        [vector_shape] * (len(vectors) + 1)
        + [near_shape, payload_shape, small_shape],
    )
    if first:
        return results[0], direction, *results[1:]
    return results


def end(sweep, scalars, wide, base, near, residual, direction, image, count):
    return call(
        end_kernel,
        "end",
        (*sweep, scalars, wide, base, near, residual, direction, image),
        [vector_shape] * 2 + [small_shape, jax.ShapeDtypeStruct((count, COLS), F32)],
    )


def per_device(
    count,
    points,
    tree_order,
    leaf_basis,
    local_transfer,
    local_coupling,
    device_transfer,
    device_coupling,
    solution,
    residual,
    direction,
):
    routes = partners(count)
    other = []
    for level in range(LEVELS - 1):
        matrix = local_transfer[6] if level == 0 else device_transfer[0, level - 1]
        other.append(lax.ppermute(matrix, "leaf", routes[level]))
    kernels = make_kernels(points, tree_order)
    wide, tall, mix, down = compose(
        leaf_basis, local_transfer, local_coupling, device_transfer, device_coupling
    )
    base, near, payload = begin(residual, direction, kernels, tall, mix)
    up = flip(local_transfer, device_transfer, other)
    image = direction
    scalars = jnp.ones((8, COLS), F32)
    for step in range(ITERATIONS):
        field = None
        for level in range(LEVELS - 1):
            got = lax.ppermute(payload, "leaf", routes[level])
            payload, field = climb(level, payload, got, up, down, field)
        got = lax.ppermute(payload, "leaf", routes[LEVELS - 1])
        sweep = (payload, got, down, field)
        if step + 1 < ITERATIONS:
            residual, direction, image, base, near, payload, scalars = turn(
                step == 0,
                sweep,
                scalars,
                wide,
                base,
                near,
                residual,
                direction,
                image,
                kernels,
                tall,
                mix,
            )
        else:
            residual, direction, scalars, spread = end(
                sweep, scalars, wide, base, near, residual, direction, image, count
            )
        solution = solution + scalars[2:3] * direction
    parts = lax.all_to_all(spread, "leaf", 0, 0, tiled=True)
    norm = jnp.sum(parts, axis=0, keepdims=True)
    direction = residual + norm / scalars[0:1] * direction
    return (solution, residual, direction)


def solution(mesh):
    placed = (
        P(None, "leaf"),
        P("leaf", None),
        P("leaf", None, None),
        P("leaf", None, None),
        P("leaf", None, None),
        P("leaf", None, None, None),
        P("leaf", None, None, None),
        P("leaf", None),
        P("leaf", None),
        P("leaf", None),
    )
    return jax.shard_map(
        functools.partial(per_device, mesh.shape["leaf"]),
        mesh=mesh,
        in_specs=placed,
        out_specs=(P("leaf", None), P("leaf", None), P("leaf", None)),
        check_vma=False,
    )
```

```python
import functools

import jax
import jax.numpy as jnp
from jax import lax
from jax.experimental import pallas as pl
from jax.experimental.pallas import tpu as pltpu
from jax.sharding import PartitionSpec as P

ITERATIONS = 3
ridge_weight = 32.0
sharpness = 0.25
LEAVES = 4
ROWS = 512
RANK = 256
COLS = 128
LEVELS = 8
PAYLOAD = RANK + 16
BF = jnp.bfloat16
F32 = jnp.float32


def dot(left, right):
    return jnp.dot(left, right, preferred_element_type=F32)


def params(size=16 << 20):
    return pltpu.CompilerParams(vmem_limit_bytes=size)


in_vmem = pl.BlockSpec(memory_space=pltpu.VMEM)


def whole(shape):
    return pl.BlockSpec(shape, lambda *_: (0,) * len(shape))


def partners(count):
    turn = {0: 6, 1: 7, 2: 4, 3: 5, 4: 2, 5: 3, 6: 0, 7: 1}
    levels = []
    for level in range(count.bit_length() - 1):
        pairs = []
        for i in range(count):
            if level == 3:
                j = i & ~14 | turn[i >> 1 & 7] << 1
            elif level in (5, 7):
                j = i ^ 3 << level - 1
            else:
                j = i ^ 1 << level
            pairs.append((i, j))
        levels.append(pairs)
    return levels


def split3(value):
    high = value.astype(BF)
    rest = value - high.astype(F32)
    mid = rest.astype(BF)
    low = (rest - mid.astype(F32)).astype(BF)
    return high, mid, low


def pack_sums(sums):
    high, mid, _ = split3(sums)
    return jnp.concatenate([high.astype(F32), mid.astype(F32)], axis=0).astype(BF)


def unpack_sums(packed):
    wide = packed.astype(F32)
    return wide[0:8] + wide[8:16]


def row_of(sums, index):
    return sums[index : index + 1]


def stack_rows(*rows):
    place = lax.broadcasted_iota(jnp.int32, (8, COLS), 0)
    total = jnp.zeros((8, COLS), F32)
    for index, row in enumerate(rows):
        total = total + jnp.where(place == index, row, 0.0)
    return total


def call(kernel, name, operands, shapes):
    return pl.pallas_call(
        kernel,
        in_specs=[in_vmem] * len(operands),
        out_specs=[in_vmem] * len(shapes),
        out_shape=shapes,
        compiler_params=params(),
        name=name,
    )(*operands)


def rows8(*rows):
    place = lax.broadcasted_iota(jnp.int32, (8, rows[0].shape[1]), 0)
    block = jnp.zeros(place.shape, F32)
    for index, row in enumerate(rows):
        block = block + jnp.where(place == index, row, 0.0)
    return block


def leaf_kernel(points_ref, order_ref, out_ref):
    value = points_ref[...]
    total = value.shape[1]
    gap = jnp.zeros((4, total), F32)
    pieces = []
    for piece in split3(value):
        pieces += [piece.astype(F32), gap]
    pieces = jnp.concatenate(pieces, axis=0).astype(BF)
    place = lax.broadcasted_iota(jnp.int32, (total, ROWS), 0)
    for i in range(LEAVES):
        picked = order_ref[:, i * ROWS : (i + 1) * ROWS]
        chosen = jnp.where(place == picked, 1.0, 0.0).astype(BF)
        moved = dot(pieces, chosen)
        high, mid, low = moved[0:32], moved[32:64], moved[64:96]
        full = high + mid + low
        half = -0.5 * jnp.sum(full * full, axis=0, keepdims=True)
        h3, m3, l3 = (piece.astype(F32) for piece in split3(half))
        one = jnp.ones_like(half)
        pad = jnp.zeros((8, ROWS), F32)
        left = jnp.concatenate(
            [high, high, mid, high, low, mid, rows8(h3, m3, l3, one, one, one), pad], axis=0
        ).astype(BF)
        right = jnp.concatenate(
            [high, mid, high, low, high, mid, rows8(one, one, one, h3, m3, l3), pad], axis=0
        ).astype(BF)
        inner = lax.dot_general(
            left, right, (((0,), (0,)), ((), ())), preferred_element_type=F32
        )
        out_ref[i] = jnp.exp((2.0 * sharpness) * inner).astype(BF)


def make_kernels(points, order):
    total = points.shape[1]
    return pl.pallas_call(
        leaf_kernel,
        in_specs=[in_vmem, in_vmem],
        out_specs=in_vmem,
        out_shape=jax.ShapeDtypeStruct((LEAVES, ROWS, ROWS), BF),
        compiler_params=params(),
        cost_estimate=pl.CostEstimate(
            flops=2 * LEAVES * (96 * total + 208 * ROWS) * ROWS,
            bytes_accessed=4 << 20,
            transcendentals=LEAVES * ROWS * ROWS,
        ),
        name="leaf_kernels",
    )(points, order)


def compose_kernel(basis, local_r, local_b, tall, mix, paths):
    first = [local_r[i] for i in range(LEAVES)]
    second = [local_r[LEAVES], local_r[LEAVES + 1]]
    flipped = [block.T for block in first]
    pair = local_b[2]
    across = [pair, pair.T]
    below = LEAVES * RANK
    for i in range(LEAVES):
        tall[i] = basis[i].T
        path = dot(first[i], second[i // 2]).astype(BF)
        paths[i * RANK : (i + 1) * RANK] = path
        mix[below:, i * RANK : (i + 1) * RANK] = path.T
        side = dot(first[i], across[i // 2]).astype(BF)
        for j in range(LEAVES):
            if i == j:
                block = jnp.zeros((RANK, RANK), BF)
            elif i // 2 == j // 2:
                block = local_b[i // 2]
                if i % 2:
                    block = block.T
            else:
                block = dot(side, flipped[j]).astype(BF)
            mix[i * RANK : (i + 1) * RANK, j * RANK : (j + 1) * RANK] = block


def compose(basis, local_r, local_b):
    shapes = [
        (LEAVES, RANK, ROWS),
        ((LEAVES + 1) * RANK, LEAVES * RANK),
        (LEAVES * RANK, RANK),
    ]
    return call(
        compose_kernel,
        "compose",
        (basis, local_r, local_b),
        [jax.ShapeDtypeStruct(shape, BF) for shape in shapes],
    )


def descend_kernel(local_r, device_r, device_b, down):
    path = None
    for level in range(LEVELS):
        coupling = device_b[0, level]
        down[level, :RANK, :] = coupling
        if path is None:
            down[level, RANK:, :] = coupling
        else:
            down[level, RANK:, :] = dot(path, coupling).astype(BF)
        if level + 1 < LEVELS:
            step = local_r[LEAVES + 2] if level == 0 else device_r[0, level - 1]
            path = step if path is None else dot(path, step).astype(BF)


def descend(local_r, device_r, device_b):
    return call(
        descend_kernel,
        "descend",
        (local_r, device_r, device_b),
        [jax.ShapeDtypeStruct((LEVELS, 2 * RANK, RANK), BF)],
    )[0]


def flip_kernel(local_r, device_r, *rest):
    out = rest[-1]
    for level in range(LEVELS - 1):
        step = local_r[LEAVES + 2] if level == 0 else device_r[0, level - 1]
        out[level, :, :RANK] = step.T
        out[level, :, RANK:] = rest[level][...].T


def flip(local_r, device_r, other_r):
    return pl.pallas_call(
        flip_kernel,
        in_specs=[in_vmem] * (2 + len(other_r)),
        out_specs=in_vmem,
        out_shape=jax.ShapeDtypeStruct((LEVELS - 1, RANK, 2 * RANK), BF),
        compiler_params=params(),
        name="flip",
    )(local_r, device_r, *other_r)


def climb_kernel(level, own, got, up, down, *rest):
    field_in = rest[0] if level else None
    out, field_out = rest[-2:]
    mine = own[:RANK]
    theirs = got[:RANK]
    out[:RANK] = dot(up[level], jnp.concatenate([mine, theirs], axis=0)).astype(BF)
    felt = dot(down[level], theirs)
    energy = jnp.sum(mine.astype(F32) * felt[:RANK], axis=0, keepdims=True)
    zero = jnp.zeros_like(energy)
    sums = unpack_sums(own[RANK:]) + unpack_sums(got[RANK:])
    out[RANK:] = pack_sums(sums + stack_rows(zero, 2.0 * energy))
    if level:
        field_out[...] = field_in[...] + felt[RANK:]
    else:
        field_out[...] = felt[RANK:]


def climb(level, own, got, up, down, field):
    operands = [own, got, up, down] + ([field] if level else [])
    return pl.pallas_call(
        functools.partial(climb_kernel, level),
        in_specs=[in_vmem] * len(operands),
        out_specs=[in_vmem] * 2,
        out_shape=[payload_shape, field_shape],
        compiler_params=params(4 << 20),
        name="climb",
    )(*operands)


def finish_sweep(own, got, down, field_in, scalars_in, first):
    mine = own[:RANK]
    theirs = got[:RANK]
    felt = dot(down[LEVELS - 1], theirs)
    field = (field_in[...] + felt[RANK:]).astype(BF)
    energy = jnp.sum(mine.astype(F32) * felt[:RANK], axis=0, keepdims=True)
    sums = unpack_sums(own[RANK:]) + unpack_sums(got[RANK:])
    norm = row_of(sums, 0)
    curve = row_of(sums, 1) + 2.0 * energy
    if first:
        return field, norm, curve, norm / curve, None
    turn = norm / scalars_in[0:1]
    bend = curve + turn * (2.0 * row_of(sums, 2) + turn * scalars_in[1:2])
    return field, norm, bend, norm / bend, turn


def column_sum(value):
    return jnp.sum(value, axis=0, keepdims=True)


def leaf_apply(vector, kernel, tall):
    low = vector.astype(BF)
    return dot(kernel, low) + ridge_weight * vector, dot(tall, low).astype(BF)


def close_leaves(mix, gathered, sums, near, payload):
    packed = jnp.concatenate(gathered, axis=0)
    below = LEAVES * RANK
    payload[:RANK] = dot(mix[below:], packed).astype(BF)
    felt = dot(mix[:below], packed)
    energy = column_sum(packed.astype(F32) * felt)
    near[...] = felt
    payload[RANK:] = pack_sums(sums + stack_rows(jnp.zeros_like(energy), energy))


def begin_kernel(residual, direction, kernel, tall, mix, base, near, payload):
    sums = None
    gathered = []
    for i in range(LEAVES):
        rows = slice(i * ROWS, (i + 1) * ROWS)
        vector = direction[rows]
        out, local = leaf_apply(vector, kernel[i], tall[i])
        base[rows] = out
        here = residual[rows]
        part = stack_rows(column_sum(here * here), column_sum(vector * out))
        sums = part if i == 0 else sums + part
        gathered.append(local)
    close_leaves(mix, gathered, sums, near, payload)


def leaf_fields(paths, near, field):
    every = (near[...] + dot(paths[...], field)).astype(BF)
    return [every[i * RANK : (i + 1) * RANK] for i in range(LEAVES)]


def turn_kernel(first, own, got, down, field_in, scalars_in, *rest):
    basis, paths, base_in, near_in = rest[:4]
    rest = rest[4:]
    if first:
        residual, image, kernel, tall, mix = rest[:5]
        residual_out, image_out, base, near, payload, scalars = rest[5:]
    else:
        residual, direction, image, kernel, tall, mix = rest[:6]
        residual_out, direction_out, image_out, base, near, payload, scalars = rest[6:]
    field, norm, bend, size, beta = finish_sweep(own, got, down, field_in, scalars_in, first)
    scalars[...] = stack_rows(norm, bend, size)
    fields = leaf_fields(paths, near_in, field)
    sums = None
    gathered = []
    for i in range(LEAVES):
        rows = slice(i * ROWS, (i + 1) * ROWS)
        pushed = base_in[rows] + dot(basis[i], fields[i])
        here = residual[rows]
        if not first:
            pushed = pushed + beta * image[rows]
            direction_out[rows] = here + beta * direction[rows]
        here = here - size * pushed
        residual_out[rows] = here
        image_out[rows] = pushed
        out, local = leaf_apply(here, kernel[i], tall[i])
        base[rows] = out
        part = stack_rows(column_sum(here * here), column_sum(here * out), column_sum(here * pushed))
        sums = part if i == 0 else sums + part
        gathered.append(local)
    close_leaves(mix, gathered, sums, near, payload)


def end_kernel(
    own,
    got,
    down,
    field_in,
    scalars_in,
    basis,
    paths,
    base_in,
    near_in,
    residual,
    direction,
    image,
    solved,
    residual_out,
    residual_kept,
    direction_out,
    solved_out,
    scalars,
    sums_out,
):
    field, norm, bend, size, beta = finish_sweep(own, got, down, field_in, scalars_in, False)
    scalars[...] = stack_rows(norm, bend, size)
    fields = leaf_fields(paths, near_in, field)
    sums = None
    for i in range(LEAVES):
        rows = slice(i * ROWS, (i + 1) * ROWS)
        pushed = base_in[rows] + dot(basis[i], fields[i])
        pushed = pushed + beta * image[rows]
        here = residual[rows]
        step = here + beta * direction[rows]
        direction_out[rows] = step
        solved_out[rows] = solved[rows] + size * step
        here = here - size * pushed
        residual_out[rows] = here
        residual_kept[rows] = here
        part = column_sum(here * here)
        sums = part if i == 0 else sums + part
    sums_out[...] = jnp.broadcast_to(sums, sums_out.shape)


def last_kernel(parts, residual, direction, scalars, out):
    beta = column_sum(parts[...]) / scalars[0:1]
    out[...] = residual[...] + beta * direction[...]


vector_shape = jax.ShapeDtypeStruct((LEAVES * ROWS, COLS), F32)
near_shape = jax.ShapeDtypeStruct((LEAVES * RANK, COLS), F32)
payload_shape = jax.ShapeDtypeStruct((PAYLOAD, COLS), BF)
field_shape = jax.ShapeDtypeStruct((RANK, COLS), F32)
small_shape = jax.ShapeDtypeStruct((8, COLS), F32)


def begin(residual, direction, kernels, tall, mix):
    return call(
        begin_kernel,
        "begin",
        (residual, direction, kernels, tall, mix),
        [vector_shape, near_shape, payload_shape],
    )


def turn(first, sweep, scalars, leaves, residual, direction, image, apply):
    vectors = (residual, image) if first else (residual, direction, image)
    results = call(
        functools.partial(turn_kernel, first),
        "turn",
        (*sweep, scalars, *leaves, *vectors, *apply),
        [vector_shape] * (len(vectors) + 1) + [near_shape, payload_shape, small_shape],
    )
    if first:
        return results[0], direction, *results[1:]
    return results


def end(sweep, scalars, leaves, residual, direction, image, solved, count):
    return call(
        end_kernel,
        "end",
        (*sweep, scalars, *leaves, residual, direction, image, solved),
        [vector_shape] * 4 + [small_shape, jax.ShapeDtypeStruct((count, COLS), F32)],
    )


def per_device(
    count,
    points,
    tree_order,
    leaf_basis,
    local_transfer,
    local_coupling,
    device_transfer,
    device_coupling,
    solution,
    residual,
    direction,
):
    routes = partners(count)
    other = []
    for level in range(LEVELS - 1):
        matrix = local_transfer[6] if level == 0 else device_transfer[0, level - 1]
        other.append(lax.ppermute(matrix, "leaf", routes[level]))
    kernels = make_kernels(points, tree_order)
    tall, mix, paths = compose(leaf_basis, local_transfer, local_coupling)
    apply = (kernels, tall, mix)
    base, near, payload = begin(residual, direction, *apply)
    down = descend(local_transfer, device_transfer, device_coupling)
    up = flip(local_transfer, device_transfer, other)
    image = direction
    scalars = jnp.ones((8, COLS), F32)
    for step in range(ITERATIONS):
        field = None
        for level in range(LEVELS - 1):
            got = lax.ppermute(payload, "leaf", routes[level])
            payload, field = climb(level, payload, got, up, down, field)
        got = lax.ppermute(payload, "leaf", routes[LEVELS - 1])
        sweep = (payload, got, down, field)
        leaves = (leaf_basis, paths, base, near)
        if step + 1 < ITERATIONS:
            residual, direction, image, base, near, payload, scalars = turn(
                step == 0, sweep, scalars, leaves, residual, direction, image, apply
            )
            solution = solution + scalars[2:3] * direction
        else:
            residual, kept, direction, solution, scalars, sums = end(
                sweep, scalars, leaves, residual, direction, image, solution, count // 2
            )
    chip = sums + lax.ppermute(sums[0:1], "leaf", routes[0])
    same_core = [list(range(core, count, 2)) for core in range(2)]
    parts = lax.all_to_all(chip, "leaf", 0, 0, axis_index_groups=same_core, tiled=True)
    direction = call(last_kernel, "last", (parts, kept, direction, scalars), [vector_shape])[0]
    return (solution, residual, direction)


def solution(mesh):
    placed = (
        P(None, "leaf"),
        P("leaf", None),
        P("leaf", None, None),
        P("leaf", None, None),
        P("leaf", None, None),
        P("leaf", None, None, None),
        P("leaf", None, None, None),
        P("leaf", None),
        P("leaf", None),
        P("leaf", None),
    )
    return jax.shard_map(
        functools.partial(per_device, mesh.shape["leaf"]),
        mesh=mesh,
        in_specs=placed,
        out_specs=(P("leaf", None), P("leaf", None), P("leaf", None)),
        check_vma=False,
    )
```

```python
import functools

import jax
import jax.numpy as jnp
from jax import lax
from jax.experimental import pallas as pl
from jax.experimental.pallas import tpu as pltpu
from jax.sharding import PartitionSpec as P

ITERATIONS = 3
ridge_weight = 32.0
sharpness = 0.25
LEAVES = 4
ROWS = 512
RANK = 256
COLS = 128
LEVELS = 8
PAYLOAD = RANK + 16
BF = jnp.bfloat16
F32 = jnp.float32


def dot(left, right):
    return jnp.dot(left, right, preferred_element_type=F32)


def params(size=16 << 20):
    return pltpu.CompilerParams(vmem_limit_bytes=size)


in_vmem = pl.BlockSpec(memory_space=pltpu.VMEM)


def whole(shape):
    return pl.BlockSpec(shape, lambda *_: (0,) * len(shape))


def partners(count):
    turn = {0: 6, 1: 7, 2: 4, 3: 5, 4: 2, 5: 3, 6: 0, 7: 1}
    levels = []
    for level in range(count.bit_length() - 1):
        pairs = []
        for i in range(count):
            if level == 3:
                j = i & ~14 | turn[i >> 1 & 7] << 1
            elif level in (5, 7):
                j = i ^ 3 << level - 1
            else:
                j = i ^ 1 << level
            pairs.append((i, j))
        levels.append(pairs)
    return levels


def split3(value):
    high = value.astype(BF)
    rest = value - high.astype(F32)
    mid = rest.astype(BF)
    low = (rest - mid.astype(F32)).astype(BF)
    return high, mid, low


def pack_sums(sums):
    high, mid, _ = split3(sums)
    return jnp.concatenate([high.astype(F32), mid.astype(F32)], axis=0).astype(BF)


def unpack_sums(packed):
    wide = packed.astype(F32)
    return wide[0:8] + wide[8:16]


def row_of(sums, index):
    return sums[index : index + 1]


def stack_rows(*rows):
    place = lax.broadcasted_iota(jnp.int32, (8, COLS), 0)
    total = jnp.zeros((8, COLS), F32)
    for index, row in enumerate(rows):
        total = total + jnp.where(place == index, row, 0.0)
    return total


def call(kernel, name, operands, shapes):
    return pl.pallas_call(
        kernel,
        in_specs=[in_vmem] * len(operands),
        out_specs=[in_vmem] * len(shapes),
        out_shape=shapes,
        compiler_params=params(),
        name=name,
    )(*operands)


def rows8(*rows):
    place = lax.broadcasted_iota(jnp.int32, (8, rows[0].shape[1]), 0)
    block = jnp.zeros(place.shape, F32)
    for index, row in enumerate(rows):
        block = block + jnp.where(place == index, row, 0.0)
    return block


def leaf_kernel(points_ref, order_ref, out_ref):
    value = points_ref[...]
    total = value.shape[1]
    gap = jnp.zeros((4, total), F32)
    pieces = []
    for piece in split3(value):
        pieces += [piece.astype(F32), gap]
    pieces = jnp.concatenate(pieces, axis=0).astype(BF)
    place = lax.broadcasted_iota(jnp.int32, (total, ROWS), 0)
    for i in range(LEAVES):
        picked = order_ref[:, i * ROWS : (i + 1) * ROWS]
        chosen = jnp.where(place == picked, 1.0, 0.0).astype(BF)
        moved = dot(pieces, chosen)
        high, mid, low = moved[0:32], moved[32:64], moved[64:96]
        full = high + mid + low
        half = -0.5 * jnp.sum(full * full, axis=0, keepdims=True)
        h3, m3, l3 = (piece.astype(F32) for piece in split3(half))
        one = jnp.ones_like(half)
        pad = jnp.zeros((8, ROWS), F32)
        left = jnp.concatenate(
            [high, high, mid, high, low, mid, rows8(h3, m3, l3, one, one, one), pad], axis=0
        ).astype(BF)
        right = jnp.concatenate(
            [high, mid, high, low, high, mid, rows8(one, one, one, h3, m3, l3), pad], axis=0
        ).astype(BF)
        inner = lax.dot_general(
            left, right, (((0,), (0,)), ((), ())), preferred_element_type=F32
        )
        out_ref[i] = jnp.exp((2.0 * sharpness) * inner).astype(BF)


def make_kernels(points, order):
    total = points.shape[1]
    return pl.pallas_call(
        leaf_kernel,
        in_specs=[in_vmem, in_vmem],
        out_specs=in_vmem,
        out_shape=jax.ShapeDtypeStruct((LEAVES, ROWS, ROWS), BF),
        compiler_params=params(),
        cost_estimate=pl.CostEstimate(
            flops=2 * LEAVES * (96 * total + 208 * ROWS) * ROWS,
            bytes_accessed=4 << 20,
            transcendentals=LEAVES * ROWS * ROWS,
        ),
        name="leaf_kernels",
    )(points, order)


def compose_kernel(basis, local_r, local_b, device_r, _, tall, mix, paths, *steps):
    for level in range(LEVELS - 1):
        step = local_r[LEAVES + 2] if level == 0 else device_r[0, level - 1]
        steps[level][...] = step.T
    first = [local_r[i] for i in range(LEAVES)]
    second = [local_r[LEAVES], local_r[LEAVES + 1]]
    flipped = [block.T for block in first]
    pair = local_b[2]
    across = [pair, pair.T]
    below = LEAVES * RANK
    for i in range(LEAVES):
        tall[i] = basis[i].T
        path = dot(first[i], second[i // 2]).astype(BF)
        paths[i * RANK : (i + 1) * RANK] = path
        mix[below:, i * RANK : (i + 1) * RANK] = path.T
        side = dot(first[i], across[i // 2]).astype(BF)
        for j in range(LEAVES):
            if i == j:
                block = jnp.zeros((RANK, RANK), BF)
            elif i // 2 == j // 2:
                block = local_b[i // 2]
                if i % 2:
                    block = block.T
            else:
                block = dot(side, flipped[j]).astype(BF)
            mix[i * RANK : (i + 1) * RANK, j * RANK : (j + 1) * RANK] = block


def compose(basis, local_r, local_b, device_r, after):
    shapes = [
        (LEAVES, RANK, ROWS),
        ((LEAVES + 1) * RANK, LEAVES * RANK),
        (LEAVES * RANK, RANK),
    ] + [(RANK, RANK)] * (LEVELS - 1)
    return pl.pallas_call(
        compose_kernel,
        in_specs=[in_vmem] * 4 + [pl.BlockSpec(memory_space=pl.ANY)],
        out_specs=[in_vmem] * len(shapes),
        out_shape=[jax.ShapeDtypeStruct(shape, BF) for shape in shapes],
        compiler_params=params(),
        name="compose",
    )(basis, local_r, local_b, device_r, after)


def descend_kernel(local_r, device_r, device_b, down):
    path = None
    for level in range(LEVELS):
        coupling = device_b[0, level]
        down[level, :RANK, :] = coupling
        if path is None:
            down[level, RANK:, :] = coupling
        else:
            down[level, RANK:, :] = dot(path, coupling).astype(BF)
        if level + 1 < LEVELS:
            step = local_r[LEAVES + 2] if level == 0 else device_r[0, level - 1]
            path = step if path is None else dot(path, step).astype(BF)


def descend(local_r, device_r, device_b):
    return call(
        descend_kernel,
        "descend",
        (local_r, device_r, device_b),
        [jax.ShapeDtypeStruct((LEVELS, 2 * RANK, RANK), BF)],
    )[0]


def climb_kernel(level, own, got, step, other, down, *rest):
    field_in = rest[0] if level else None
    out, field_out = rest[-2:]
    mine = own[:RANK]
    theirs = got[:RANK]
    out[:RANK] = (dot(step[...], mine) + dot(other[...], theirs)).astype(BF)
    felt = dot(down[level], theirs)
    energy = jnp.sum(mine.astype(F32) * felt[:RANK], axis=0, keepdims=True)
    zero = jnp.zeros_like(energy)
    sums = unpack_sums(own[RANK:]) + unpack_sums(got[RANK:])
    out[RANK:] = pack_sums(sums + stack_rows(zero, 2.0 * energy))
    if level:
        field_out[...] = field_in[...] + felt[RANK:]
    else:
        field_out[...] = felt[RANK:]


def climb(level, own, got, step, other, down, field):
    operands = [own, got, step, other, down] + ([field] if level else [])
    return pl.pallas_call(
        functools.partial(climb_kernel, level),
        in_specs=[in_vmem] * len(operands),
        out_specs=[in_vmem] * 2,
        out_shape=[payload_shape, field_shape],
        compiler_params=params(4 << 20),
        name="climb",
    )(*operands)


def finish_sweep(own, got, down, field_in, scalars_in, first):
    mine = own[:RANK]
    theirs = got[:RANK]
    felt = dot(down[LEVELS - 1], theirs)
    field = (field_in[...] + felt[RANK:]).astype(BF)
    energy = jnp.sum(mine.astype(F32) * felt[:RANK], axis=0, keepdims=True)
    sums = unpack_sums(own[RANK:]) + unpack_sums(got[RANK:])
    norm = row_of(sums, 0)
    curve = row_of(sums, 1) + 2.0 * energy
    if first:
        return field, norm, curve, norm / curve, None
    turn = norm / scalars_in[0:1]
    bend = curve + turn * (2.0 * row_of(sums, 2) + turn * scalars_in[1:2])
    return field, norm, bend, norm / bend, turn


def column_sum(value):
    return jnp.sum(value, axis=0, keepdims=True)


def leaf_apply(vector, kernel, tall):
    low = vector.astype(BF)
    return dot(kernel, low) + ridge_weight * vector, dot(tall, low).astype(BF)


def close_leaves(mix, gathered, sums, near, payload):
    packed = jnp.concatenate(gathered, axis=0)
    below = LEAVES * RANK
    payload[:RANK] = dot(mix[below:], packed).astype(BF)
    felt = dot(mix[:below], packed)
    energy = column_sum(packed.astype(F32) * felt)
    near[...] = felt
    payload[RANK:] = pack_sums(sums + stack_rows(jnp.zeros_like(energy), energy))


def begin_kernel(residual, direction, kernel, tall, mix, base, near, payload):
    sums = None
    gathered = []
    for i in range(LEAVES):
        rows = slice(i * ROWS, (i + 1) * ROWS)
        vector = direction[rows]
        out, local = leaf_apply(vector, kernel[i], tall[i])
        base[rows] = out
        here = residual[rows]
        part = stack_rows(column_sum(here * here), column_sum(vector * out))
        sums = part if i == 0 else sums + part
        gathered.append(local)
    close_leaves(mix, gathered, sums, near, payload)


def leaf_fields(paths, near, field):
    every = (near[...] + dot(paths[...], field)).astype(BF)
    return [every[i * RANK : (i + 1) * RANK] for i in range(LEAVES)]


def turn_kernel(first, own, got, down, field_in, scalars_in, *rest):
    basis, paths, base_in, near_in = rest[:4]
    rest = rest[4:]
    if first:
        residual, image, kernel, tall, mix = rest[:5]
        residual_out, image_out, base, near, payload, scalars = rest[5:]
    else:
        residual, direction, image, kernel, tall, mix = rest[:6]
        residual_out, direction_out, image_out, base, near, payload, scalars = rest[6:]
    field, norm, bend, size, beta = finish_sweep(own, got, down, field_in, scalars_in, first)
    scalars[...] = stack_rows(norm, bend, size)
    fields = leaf_fields(paths, near_in, field)
    sums = None
    gathered = []
    for i in range(LEAVES):
        rows = slice(i * ROWS, (i + 1) * ROWS)
        pushed = base_in[rows] + dot(basis[i], fields[i])
        here = residual[rows]
        if not first:
            pushed = pushed + beta * image[rows]
            direction_out[rows] = here + beta * direction[rows]
        here = here - size * pushed
        residual_out[rows] = here
        image_out[rows] = pushed
        out, local = leaf_apply(here, kernel[i], tall[i])
        base[rows] = out
        part = stack_rows(column_sum(here * here), column_sum(here * out), column_sum(here * pushed))
        sums = part if i == 0 else sums + part
        gathered.append(local)
    close_leaves(mix, gathered, sums, near, payload)


def end_kernel(
    own,
    got,
    down,
    field_in,
    scalars_in,
    basis,
    paths,
    base_in,
    near_in,
    residual,
    direction,
    image,
    solved,
    residual_out,
    residual_kept,
    direction_out,
    solved_out,
    scalars,
    sums_out,
):
    field, norm, bend, size, beta = finish_sweep(own, got, down, field_in, scalars_in, False)
    scalars[...] = stack_rows(norm, bend, size)
    fields = leaf_fields(paths, near_in, field)
    sums = None
    for i in range(LEAVES):
        rows = slice(i * ROWS, (i + 1) * ROWS)
        pushed = base_in[rows] + dot(basis[i], fields[i])
        pushed = pushed + beta * image[rows]
        here = residual[rows]
        step = here + beta * direction[rows]
        direction_out[rows] = step
        solved_out[rows] = solved[rows] + size * step
        here = here - size * pushed
        residual_out[rows] = here
        residual_kept[rows] = here
        part = column_sum(here * here)
        sums = part if i == 0 else sums + part
    sums_out[...] = jnp.broadcast_to(sums, sums_out.shape)


def last_kernel(parts, residual, direction, scalars, out):
    beta = column_sum(parts[...]) / scalars[0:1]
    out[...] = residual[...] + beta * direction[...]


vector_shape = jax.ShapeDtypeStruct((LEAVES * ROWS, COLS), F32)
near_shape = jax.ShapeDtypeStruct((LEAVES * RANK, COLS), F32)
payload_shape = jax.ShapeDtypeStruct((PAYLOAD, COLS), BF)
field_shape = jax.ShapeDtypeStruct((RANK, COLS), F32)
small_shape = jax.ShapeDtypeStruct((8, COLS), F32)


def begin(residual, direction, kernels, tall, mix):
    return call(
        begin_kernel,
        "begin",
        (residual, direction, kernels, tall, mix),
        [vector_shape, near_shape, payload_shape],
    )


def turn(first, sweep, scalars, leaves, residual, direction, image, apply):
    vectors = (residual, image) if first else (residual, direction, image)
    results = call(
        functools.partial(turn_kernel, first),
        "turn",
        (*sweep, scalars, *leaves, *vectors, *apply),
        [vector_shape] * (len(vectors) + 1) + [near_shape, payload_shape, small_shape],
    )
    if first:
        return results[0], direction, *results[1:]
    return results


def end(sweep, scalars, leaves, residual, direction, image, solved, count):
    return call(
        end_kernel,
        "end",
        (*sweep, scalars, *leaves, residual, direction, image, solved),
        [vector_shape] * 4 + [small_shape, jax.ShapeDtypeStruct((count, COLS), F32)],
    )


def per_device(
    count,
    points,
    tree_order,
    leaf_basis,
    local_transfer,
    local_coupling,
    device_transfer,
    device_coupling,
    solution,
    residual,
    direction,
):
    routes = partners(count)
    kernels = make_kernels(points, tree_order)
    tall, mix, paths, *steps = compose(
        leaf_basis, local_transfer, local_coupling, device_transfer, kernels
    )
    others = [lax.ppermute(block, "leaf", route) for block, route in zip(steps, routes)]
    apply = (kernels, tall, mix)
    base, near, payload = begin(residual, direction, *apply)
    down = descend(local_transfer, device_transfer, device_coupling)
    image = direction
    scalars = jnp.ones((8, COLS), F32)
    for step in range(ITERATIONS):
        field = None
        for level in range(LEVELS - 1):
            got = lax.ppermute(payload, "leaf", routes[level])
            payload, field = climb(
                level, payload, got, steps[level], others[level], down, field
            )
        got = lax.ppermute(payload, "leaf", routes[LEVELS - 1])
        sweep = (payload, got, down, field)
        leaves = (leaf_basis, paths, base, near)
        if step + 1 < ITERATIONS:
            residual, direction, image, base, near, payload, scalars = turn(
                step == 0, sweep, scalars, leaves, residual, direction, image, apply
            )
            solution = solution + scalars[2:3] * direction
        else:
            residual, kept, direction, solution, scalars, sums = end(
                sweep, scalars, leaves, residual, direction, image, solution, count // 2
            )
    chip = sums + lax.ppermute(sums[0:1], "leaf", routes[0])
    same_core = [list(range(core, count, 2)) for core in range(2)]
    parts = lax.all_to_all(chip, "leaf", 0, 0, axis_index_groups=same_core, tiled=True)
    direction = call(last_kernel, "last", (parts, kept, direction, scalars), [vector_shape])[0]
    return (solution, residual, direction)


def solution(mesh):
    placed = (
        P(None, "leaf"),
        P("leaf", None),
        P("leaf", None, None),
        P("leaf", None, None),
        P("leaf", None, None),
        P("leaf", None, None, None),
        P("leaf", None, None, None),
        P("leaf", None),
        P("leaf", None),
        P("leaf", None),
    )
    return jax.shard_map(
        functools.partial(per_device, mesh.shape["leaf"]),
        mesh=mesh,
        in_specs=placed,
        out_specs=(P("leaf", None), P("leaf", None), P("leaf", None)),
        check_vma=False,
    )
```

```python
import functools

import jax
import jax.numpy as jnp
from jax import lax
from jax.experimental import pallas as pl
from jax.experimental.pallas import tpu as pltpu
from jax.sharding import PartitionSpec as P

ITERATIONS = 3
ridge_weight = 32.0
sharpness = 0.25
LEAVES = 4
ROWS = 512
RANK = 256
COLS = 128
LEVELS = 8
PAYLOAD = RANK + 16
BF = jnp.bfloat16
F32 = jnp.float32


def dot(left, right):
    return jnp.dot(left, right, preferred_element_type=F32)


def params(size=16 << 20):
    return pltpu.CompilerParams(vmem_limit_bytes=size)


in_vmem = pl.BlockSpec(memory_space=pltpu.VMEM)


def whole(shape):
    return pl.BlockSpec(shape, lambda *_: (0,) * len(shape))


def partners(count):
    turn = {0: 6, 1: 7, 2: 4, 3: 5, 4: 2, 5: 3, 6: 0, 7: 1}
    levels = []
    for level in range(count.bit_length() - 1):
        pairs = []
        for i in range(count):
            if level == 3:
                j = i & ~14 | turn[i >> 1 & 7] << 1
            elif level in (5, 7):
                j = i ^ 3 << level - 1
            else:
                j = i ^ 1 << level
            pairs.append((i, j))
        levels.append(pairs)
    return levels


def split3(value):
    high = value.astype(BF)
    rest = value - high.astype(F32)
    mid = rest.astype(BF)
    low = (rest - mid.astype(F32)).astype(BF)
    return high, mid, low


def pack_sums(sums):
    high, mid, _ = split3(sums)
    return jnp.concatenate([high.astype(F32), mid.astype(F32)], axis=0).astype(BF)


def unpack_sums(packed):
    wide = packed.astype(F32)
    return wide[0:8] + wide[8:16]


def row_of(sums, index):
    return sums[index : index + 1]


def stack_rows(*rows):
    place = lax.broadcasted_iota(jnp.int32, (8, COLS), 0)
    total = jnp.zeros((8, COLS), F32)
    for index, row in enumerate(rows):
        total = total + jnp.where(place == index, row, 0.0)
    return total


def call(kernel, name, operands, shapes):
    return pl.pallas_call(
        kernel,
        in_specs=[in_vmem] * len(operands),
        out_specs=[in_vmem] * len(shapes),
        out_shape=shapes,
        compiler_params=params(),
        name=name,
    )(*operands)


def rows8(*rows):
    place = lax.broadcasted_iota(jnp.int32, (8, rows[0].shape[1]), 0)
    block = jnp.zeros(place.shape, F32)
    for index, row in enumerate(rows):
        block = block + jnp.where(place == index, row, 0.0)
    return block


def leaf_kernel(points_ref, order_ref, out_ref):
    value = points_ref[...]
    total = value.shape[1]
    gap = jnp.zeros((4, total), F32)
    pieces = []
    for piece in split3(value):
        pieces += [piece.astype(F32), gap]
    pieces = jnp.concatenate(pieces, axis=0).astype(BF)
    place = lax.broadcasted_iota(jnp.int32, (total, ROWS), 0)
    for i in range(LEAVES):
        picked = order_ref[:, i * ROWS : (i + 1) * ROWS]
        chosen = jnp.where(place == picked, 1.0, 0.0).astype(BF)
        moved = dot(pieces, chosen)
        high, mid, low = moved[0:32], moved[32:64], moved[64:96]
        full = high + mid + low
        half = -0.5 * jnp.sum(full * full, axis=0, keepdims=True)
        h3, m3, l3 = (piece.astype(F32) for piece in split3(half))
        one = jnp.ones_like(half)
        pad = jnp.zeros((8, ROWS), F32)
        left = jnp.concatenate(
            [high, high, mid, high, low, mid, rows8(h3, m3, l3, one, one, one), pad], axis=0
        ).astype(BF)
        right = jnp.concatenate(
            [high, mid, high, low, high, mid, rows8(one, one, one, h3, m3, l3), pad], axis=0
        ).astype(BF)
        inner = lax.dot_general(
            left, right, (((0,), (0,)), ((), ())), preferred_element_type=F32
        )
        out_ref[i] = jnp.exp((2.0 * sharpness) * inner).astype(BF)


def make_kernels(points, order):
    total = points.shape[1]
    return pl.pallas_call(
        leaf_kernel,
        in_specs=[in_vmem, in_vmem],
        out_specs=in_vmem,
        out_shape=jax.ShapeDtypeStruct((LEAVES, ROWS, ROWS), BF),
        compiler_params=params(),
        cost_estimate=pl.CostEstimate(
            flops=2 * LEAVES * (96 * total + 208 * ROWS) * ROWS,
            bytes_accessed=4 << 20,
            transcendentals=LEAVES * ROWS * ROWS,
        ),
        name="leaf_kernels",
    )(points, order)


def compose_kernel(basis, local_r, local_b, device_r, _, tall, mix, paths, *steps):
    for level in range(LEVELS - 1):
        step = local_r[LEAVES + 2] if level == 0 else device_r[0, level - 1]
        steps[level][...] = step.T
    first = [local_r[i] for i in range(LEAVES)]
    second = [local_r[LEAVES], local_r[LEAVES + 1]]
    flipped = [block.T for block in first]
    pair = local_b[2]
    across = [pair, pair.T]
    below = LEAVES * RANK
    for i in range(LEAVES):
        tall[i] = basis[i].T
        path = dot(first[i], second[i // 2]).astype(BF)
        paths[i * RANK : (i + 1) * RANK] = path
        mix[below:, i * RANK : (i + 1) * RANK] = path.T
        side = dot(first[i], across[i // 2]).astype(BF)
        for j in range(LEAVES):
            if i == j:
                block = jnp.zeros((RANK, RANK), BF)
            elif i // 2 == j // 2:
                block = local_b[i // 2]
                if i % 2:
                    block = block.T
            else:
                block = dot(side, flipped[j]).astype(BF)
            mix[i * RANK : (i + 1) * RANK, j * RANK : (j + 1) * RANK] = block


def compose(basis, local_r, local_b, device_r, after):
    shapes = [
        (LEAVES, RANK, ROWS),
        ((LEAVES + 1) * RANK, LEAVES * RANK),
        (LEAVES * RANK, RANK),
    ] + [(RANK, RANK)] * (LEVELS - 1)
    return pl.pallas_call(
        compose_kernel,
        in_specs=[in_vmem] * 4 + [pl.BlockSpec(memory_space=pl.ANY)],
        out_specs=[in_vmem] * len(shapes),
        out_shape=[jax.ShapeDtypeStruct(shape, BF) for shape in shapes],
        compiler_params=params(),
        name="compose",
    )(basis, local_r, local_b, device_r, after)


def descend_kernel(local_r, device_r, device_b, down):
    path = None
    for level in range(LEVELS):
        coupling = device_b[0, level]
        down[level, :RANK, :] = coupling
        if path is None:
            down[level, RANK:, :] = coupling
        else:
            down[level, RANK:, :] = dot(path, coupling).astype(BF)
        if level + 1 < LEVELS:
            step = local_r[LEAVES + 2] if level == 0 else device_r[0, level - 1]
            path = step if path is None else dot(path, step).astype(BF)


def descend(local_r, device_r, device_b):
    return call(
        descend_kernel,
        "descend",
        (local_r, device_r, device_b),
        [jax.ShapeDtypeStruct((LEVELS, 2 * RANK, RANK), BF)],
    )[0]


def climb_kernel(level, own, got, step, other, down, *rest):
    field_in = rest[0] if level else None
    out, field_out = rest[-2:]
    mine = own[:RANK]
    theirs = got[:RANK]
    out[:RANK] = (dot(step[...], mine) + dot(other[...], theirs)).astype(BF)
    if level:
        felt = dot(down[level], theirs)
    else:
        felt = dot(down[0, 0], theirs)
    energy = jnp.sum(mine.astype(F32) * felt[:RANK], axis=0, keepdims=True)
    zero = jnp.zeros_like(energy)
    sums = unpack_sums(own[RANK:]) + unpack_sums(got[RANK:])
    out[RANK:] = pack_sums(sums + stack_rows(zero, 2.0 * energy))
    if level:
        field_out[...] = field_in[...] + felt[RANK:]
    else:
        field_out[...] = felt


def climb(level, own, got, step, other, down, field):
    operands = [own, got, step, other, down] + ([field] if level else [])
    return pl.pallas_call(
        functools.partial(climb_kernel, level),
        in_specs=[in_vmem] * len(operands),
        out_specs=[in_vmem] * 2,
        out_shape=[payload_shape, field_shape],
        compiler_params=params(4 << 20),
        name="climb",
    )(*operands)


def finish_sweep(own, got, down, field_in, scalars_in, first):
    mine = own[:RANK]
    theirs = got[:RANK]
    felt = dot(down[LEVELS - 1], theirs)
    field = (field_in[...] + felt[RANK:]).astype(BF)
    energy = jnp.sum(mine.astype(F32) * felt[:RANK], axis=0, keepdims=True)
    sums = unpack_sums(own[RANK:]) + unpack_sums(got[RANK:])
    norm = row_of(sums, 0)
    curve = row_of(sums, 1) + 2.0 * energy
    if first:
        return field, norm, curve, norm / curve, None
    turn = norm / scalars_in[0:1]
    bend = curve + turn * (2.0 * row_of(sums, 2) + turn * scalars_in[1:2])
    return field, norm, bend, norm / bend, turn


def column_sum(value):
    return jnp.sum(value, axis=0, keepdims=True)


def leaf_apply(vector, kernel, tall):
    low = vector.astype(BF)
    return dot(kernel, low) + ridge_weight * vector, dot(tall, low).astype(BF)


def close_leaves(mix, gathered, sums, near, payload):
    packed = jnp.concatenate(gathered, axis=0)
    below = LEAVES * RANK
    payload[:RANK] = dot(mix[below:], packed).astype(BF)
    felt = dot(mix[:below], packed)
    energy = column_sum(packed.astype(F32) * felt)
    near[...] = felt
    payload[RANK:] = pack_sums(sums + stack_rows(jnp.zeros_like(energy), energy))


def begin_kernel(residual, direction, kernel, tall, mix, base, near, payload):
    sums = None
    gathered = []
    for i in range(LEAVES):
        rows = slice(i * ROWS, (i + 1) * ROWS)
        vector = direction[rows]
        out, local = leaf_apply(vector, kernel[i], tall[i])
        base[rows] = out
        here = residual[rows]
        part = stack_rows(column_sum(here * here), column_sum(vector * out))
        sums = part if i == 0 else sums + part
        gathered.append(local)
    close_leaves(mix, gathered, sums, near, payload)


def leaf_fields(paths, near, field):
    every = (near[...] + dot(paths[...], field)).astype(BF)
    return [every[i * RANK : (i + 1) * RANK] for i in range(LEAVES)]


def turn_kernel(first, own, got, down, field_in, scalars_in, *rest):
    basis, paths, base_in, near_in = rest[:4]
    rest = rest[4:]
    if first:
        residual, image, kernel, tall, mix = rest[:5]
        residual_out, image_out, base, near, payload, scalars = rest[5:]
    else:
        residual, direction, image, kernel, tall, mix = rest[:6]
        residual_out, direction_out, image_out, base, near, payload, scalars = rest[6:]
    field, norm, bend, size, beta = finish_sweep(own, got, down, field_in, scalars_in, first)
    scalars[...] = stack_rows(norm, bend, size)
    fields = leaf_fields(paths, near_in, field)
    sums = None
    gathered = []
    for i in range(LEAVES):
        rows = slice(i * ROWS, (i + 1) * ROWS)
        pushed = base_in[rows] + dot(basis[i], fields[i])
        here = residual[rows]
        if not first:
            pushed = pushed + beta * image[rows]
            direction_out[rows] = here + beta * direction[rows]
        here = here - size * pushed
        residual_out[rows] = here
        image_out[rows] = pushed
        out, local = leaf_apply(here, kernel[i], tall[i])
        base[rows] = out
        part = stack_rows(column_sum(here * here), column_sum(here * out), column_sum(here * pushed))
        sums = part if i == 0 else sums + part
        gathered.append(local)
    close_leaves(mix, gathered, sums, near, payload)


def end_kernel(
    own,
    got,
    down,
    field_in,
    scalars_in,
    basis,
    paths,
    base_in,
    near_in,
    residual,
    direction,
    image,
    solved,
    residual_out,
    residual_kept,
    direction_out,
    solved_out,
    scalars,
    sums_out,
):
    field, norm, bend, size, beta = finish_sweep(own, got, down, field_in, scalars_in, False)
    scalars[...] = stack_rows(norm, bend, size)
    fields = leaf_fields(paths, near_in, field)
    sums = None
    for i in range(LEAVES):
        rows = slice(i * ROWS, (i + 1) * ROWS)
        pushed = base_in[rows] + dot(basis[i], fields[i])
        pushed = pushed + beta * image[rows]
        here = residual[rows]
        step = here + beta * direction[rows]
        direction_out[rows] = step
        solved_out[rows] = solved[rows] + size * step
        here = here - size * pushed
        residual_out[rows] = here
        residual_kept[rows] = here
        part = column_sum(here * here)
        sums = part if i == 0 else sums + part
    sums_out[...] = jnp.broadcast_to(sums, sums_out.shape)


def last_kernel(parts, residual, direction, scalars, out):
    beta = column_sum(parts[...]) / scalars[0:1]
    out[...] = residual[...] + beta * direction[...]


vector_shape = jax.ShapeDtypeStruct((LEAVES * ROWS, COLS), F32)
near_shape = jax.ShapeDtypeStruct((LEAVES * RANK, COLS), F32)
payload_shape = jax.ShapeDtypeStruct((PAYLOAD, COLS), BF)
field_shape = jax.ShapeDtypeStruct((RANK, COLS), F32)
small_shape = jax.ShapeDtypeStruct((8, COLS), F32)


def begin(residual, direction, kernels, tall, mix):
    return call(
        begin_kernel,
        "begin",
        (residual, direction, kernels, tall, mix),
        [vector_shape, near_shape, payload_shape],
    )


def turn(first, sweep, scalars, leaves, residual, direction, image, apply):
    vectors = (residual, image) if first else (residual, direction, image)
    results = call(
        functools.partial(turn_kernel, first),
        "turn",
        (*sweep, scalars, *leaves, *vectors, *apply),
        [vector_shape] * (len(vectors) + 1) + [near_shape, payload_shape, small_shape],
    )
    if first:
        return results[0], direction, *results[1:]
    return results


def end(sweep, scalars, leaves, residual, direction, image, solved, count):
    return call(
        end_kernel,
        "end",
        (*sweep, scalars, *leaves, residual, direction, image, solved),
        [vector_shape] * 4 + [small_shape, jax.ShapeDtypeStruct((count, COLS), F32)],
    )


def per_device(
    count,
    points,
    tree_order,
    leaf_basis,
    local_transfer,
    local_coupling,
    device_transfer,
    device_coupling,
    solution,
    residual,
    direction,
):
    routes = partners(count)
    kernels = make_kernels(points, tree_order)
    tall, mix, paths, *steps = compose(
        leaf_basis, local_transfer, local_coupling, device_transfer, kernels
    )
    others = [lax.ppermute(block, "leaf", route) for block, route in zip(steps, routes)]
    apply = (kernels, tall, mix)
    base, near, payload = begin(residual, direction, *apply)
    down = descend(local_transfer, device_transfer, device_coupling)
    image = direction
    scalars = jnp.ones((8, COLS), F32)
    for step in range(ITERATIONS):
        field = None
        for level in range(LEVELS - 1):
            got = lax.ppermute(payload, "leaf", routes[level])
            across = down if level else device_coupling
            payload, field = climb(
                level, payload, got, steps[level], others[level], across, field
            )
        got = lax.ppermute(payload, "leaf", routes[LEVELS - 1])
        sweep = (payload, got, down, field)
        leaves = (leaf_basis, paths, base, near)
        if step + 1 < ITERATIONS:
            residual, direction, image, base, near, payload, scalars = turn(
                step == 0, sweep, scalars, leaves, residual, direction, image, apply
            )
            solution = solution + scalars[2:3] * direction
        else:
            residual, kept, direction, solution, scalars, sums = end(
                sweep, scalars, leaves, residual, direction, image, solution, count // 2
            )
    chip = sums + lax.ppermute(sums[0:1], "leaf", routes[0])
    same_core = [list(range(core, count, 2)) for core in range(2)]
    parts = lax.all_to_all(chip, "leaf", 0, 0, axis_index_groups=same_core, tiled=True)
    direction = call(last_kernel, "last", (parts, kept, direction, scalars), [vector_shape])[0]
    return (solution, residual, direction)


def solution(mesh):
    placed = (
        P(None, "leaf"),
        P("leaf", None),
        P("leaf", None, None),
        P("leaf", None, None),
        P("leaf", None, None),
        P("leaf", None, None, None),
        P("leaf", None, None, None),
        P("leaf", None),
        P("leaf", None),
        P("leaf", None),
    )
    return jax.shard_map(
        functools.partial(per_device, mesh.shape["leaf"]),
        mesh=mesh,
        in_specs=placed,
        out_specs=(P("leaf", None), P("leaf", None), P("leaf", None)),
        check_vma=False,
    )
```

```python
import functools

import jax
import jax.numpy as jnp
from jax import lax
from jax.experimental import pallas as pl
from jax.experimental.pallas import tpu as pltpu
from jax.sharding import PartitionSpec as P

ITERATIONS = 3
ridge_weight = 32.0
sharpness = 0.25
LEAVES = 4
ROWS = 512
RANK = 256
COLS = 128
LEVELS = 8
PAYLOAD = RANK + 16
BF = jnp.bfloat16
F32 = jnp.float32


def dot(left, right):
    return jnp.dot(left, right, preferred_element_type=F32)


def params(size=16 << 20):
    return pltpu.CompilerParams(vmem_limit_bytes=size)


in_vmem = pl.BlockSpec(memory_space=pltpu.VMEM)


def whole(shape):
    return pl.BlockSpec(shape, lambda *_: (0,) * len(shape))


def partners(count):
    turn = {0: 6, 1: 7, 2: 4, 3: 5, 4: 2, 5: 3, 6: 0, 7: 1}
    levels = []
    for level in range(count.bit_length() - 1):
        pairs = []
        for i in range(count):
            if level == 3:
                j = i & ~14 | turn[i >> 1 & 7] << 1
            elif level in (5, 7):
                j = i ^ 3 << level - 1
            else:
                j = i ^ 1 << level
            pairs.append((i, j))
        levels.append(pairs)
    return levels


def split3(value):
    high = value.astype(BF)
    rest = value - high.astype(F32)
    mid = rest.astype(BF)
    low = (rest - mid.astype(F32)).astype(BF)
    return high, mid, low


def pack_sums(sums):
    high, mid, _ = split3(sums)
    return jnp.concatenate([high.astype(F32), mid.astype(F32)], axis=0).astype(BF)


def unpack_sums(packed):
    wide = packed.astype(F32)
    return wide[0:8] + wide[8:16]


def row_of(sums, index):
    return sums[index : index + 1]


def stack_rows(*rows):
    place = lax.broadcasted_iota(jnp.int32, (8, COLS), 0)
    total = jnp.zeros((8, COLS), F32)
    for index, row in enumerate(rows):
        total = total + jnp.where(place == index, row, 0.0)
    return total


def call(kernel, name, operands, shapes):
    return pl.pallas_call(
        kernel,
        in_specs=[in_vmem] * len(operands),
        out_specs=[in_vmem] * len(shapes),
        out_shape=shapes,
        compiler_params=params(),
        name=name,
    )(*operands)


def rows8(*rows):
    place = lax.broadcasted_iota(jnp.int32, (8, rows[0].shape[1]), 0)
    block = jnp.zeros(place.shape, F32)
    for index, row in enumerate(rows):
        block = block + jnp.where(place == index, row, 0.0)
    return block


def leaf_kernel(points_ref, order_ref, out_ref):
    value = points_ref[...]
    total = value.shape[1]
    gap = jnp.zeros((4, total), F32)
    pieces = []
    for piece in split3(value):
        pieces += [piece.astype(F32), gap]
    pieces = jnp.concatenate(pieces, axis=0).astype(BF)
    lanes = 128
    blocks = total // lanes
    height = pieces.shape[0]
    stacked = jnp.concatenate(
        [pieces[:, c * lanes : (c + 1) * lanes] for c in range(blocks)], axis=0
    )
    place = lax.broadcasted_iota(jnp.int32, (lanes, ROWS), 0)
    for i in range(LEAVES):
        picked = order_ref[:, i * ROWS : (i + 1) * ROWS]
        chosen = jnp.where(place == (picked & (lanes - 1)), 1.0, 0.0).astype(BF)
        found = dot(stacked, chosen)
        block = picked >> 7
        moved = jnp.zeros((height, ROWS), F32)
        for c in range(blocks):
            part = found[c * height : (c + 1) * height]
            moved = moved + part * jnp.where(block == c, 1.0, 0.0)
        high, mid, low = moved[0:32], moved[32:64], moved[64:96]
        full = high + mid + low
        half = -0.5 * jnp.sum(full * full, axis=0, keepdims=True)
        h3, m3, l3 = (piece.astype(F32) for piece in split3(half))
        one = jnp.ones_like(half)
        pad = jnp.zeros((8, ROWS), F32)
        left = jnp.concatenate(
            [high, high, mid, high, low, mid, rows8(h3, m3, l3, one, one, one), pad], axis=0
        ).astype(BF)
        right = jnp.concatenate(
            [high, mid, high, low, high, mid, rows8(one, one, one, h3, m3, l3), pad], axis=0
        ).astype(BF)
        inner = lax.dot_general(
            left, right, (((0,), (0,)), ((), ())), preferred_element_type=F32
        )
        out_ref[i] = jnp.exp((2.0 * sharpness) * inner).astype(BF)


def make_kernels(points, order):
    total = points.shape[1]
    return pl.pallas_call(
        leaf_kernel,
        in_specs=[in_vmem, in_vmem],
        out_specs=in_vmem,
        out_shape=jax.ShapeDtypeStruct((LEAVES, ROWS, ROWS), BF),
        compiler_params=params(),
        cost_estimate=pl.CostEstimate(
            flops=2 * LEAVES * (96 * total + 208 * ROWS) * ROWS,
            bytes_accessed=4 << 20,
            transcendentals=LEAVES * ROWS * ROWS,
        ),
        name="leaf_kernels",
    )(points, order)


def compose_kernel(basis, local_r, local_b, device_r, _, tall, mix, paths, *steps):
    for level in range(LEVELS - 1):
        step = local_r[LEAVES + 2] if level == 0 else device_r[0, level - 1]
        steps[level][...] = step.T
    first = [local_r[i] for i in range(LEAVES)]
    second = [local_r[LEAVES], local_r[LEAVES + 1]]
    flipped = [block.T for block in first]
    pair = local_b[2]
    across = [pair, pair.T]
    below = LEAVES * RANK
    for i in range(LEAVES):
        tall[i] = basis[i].T
        path = dot(first[i], second[i // 2]).astype(BF)
        paths[i * RANK : (i + 1) * RANK] = path
        mix[below:, i * RANK : (i + 1) * RANK] = path.T
        side = dot(first[i], across[i // 2]).astype(BF)
        for j in range(LEAVES):
            if i == j:
                block = jnp.zeros((RANK, RANK), BF)
            elif i // 2 == j // 2:
                block = local_b[i // 2]
                if i % 2:
                    block = block.T
            else:
                block = dot(side, flipped[j]).astype(BF)
            mix[i * RANK : (i + 1) * RANK, j * RANK : (j + 1) * RANK] = block


def compose(basis, local_r, local_b, device_r, after):
    shapes = [
        (LEAVES, RANK, ROWS),
        ((LEAVES + 1) * RANK, LEAVES * RANK),
        (LEAVES * RANK, RANK),
    ] + [(RANK, RANK)] * (LEVELS - 1)
    return pl.pallas_call(
        compose_kernel,
        in_specs=[in_vmem] * 4 + [pl.BlockSpec(memory_space=pl.ANY)],
        out_specs=[in_vmem] * len(shapes),
        out_shape=[jax.ShapeDtypeStruct(shape, BF) for shape in shapes],
        compiler_params=params(),
        name="compose",
    )(basis, local_r, local_b, device_r, after)


def descend_kernel(local_r, device_r, device_b, down):
    path = None
    for level in range(LEVELS):
        coupling = device_b[0, level]
        down[level, :RANK, :] = coupling
        if path is None:
            down[level, RANK:, :] = coupling
        else:
            down[level, RANK:, :] = dot(path, coupling).astype(BF)
        if level + 1 < LEVELS:
            step = local_r[LEAVES + 2] if level == 0 else device_r[0, level - 1]
            path = step if path is None else dot(path, step).astype(BF)


def descend(local_r, device_r, device_b):
    return call(
        descend_kernel,
        "descend",
        (local_r, device_r, device_b),
        [jax.ShapeDtypeStruct((LEVELS, 2 * RANK, RANK), BF)],
    )[0]


def climb_kernel(level, own, got, step, other, down, *rest):
    field_in = rest[0] if level else None
    out, field_out = rest[-2:]
    mine = own[:RANK]
    theirs = got[:RANK]
    out[:RANK] = (dot(step[...], mine) + dot(other[...], theirs)).astype(BF)
    felt = dot(down[level], theirs)
    energy = jnp.sum(mine.astype(F32) * felt[:RANK], axis=0, keepdims=True)
    zero = jnp.zeros_like(energy)
    sums = unpack_sums(own[RANK:]) + unpack_sums(got[RANK:])
    out[RANK:] = pack_sums(sums + stack_rows(zero, 2.0 * energy))
    if level:
        field_out[...] = field_in[...] + felt[RANK:]
    else:
        field_out[...] = felt[RANK:]


def climb(level, own, got, step, other, down, field):
    operands = [own, got, step, other, down] + ([field] if level else [])
    return pl.pallas_call(
        functools.partial(climb_kernel, level),
        in_specs=[in_vmem] * len(operands),
        out_specs=[in_vmem] * 2,
        out_shape=[payload_shape, field_shape],
        compiler_params=params(4 << 20),
        name="climb",
    )(*operands)


def finish_sweep(own, got, down, field_in, scalars_in, first):
    mine = own[:RANK]
    theirs = got[:RANK]
    felt = dot(down[LEVELS - 1], theirs)
    field = (field_in[...] + felt[RANK:]).astype(BF)
    energy = jnp.sum(mine.astype(F32) * felt[:RANK], axis=0, keepdims=True)
    sums = unpack_sums(own[RANK:]) + unpack_sums(got[RANK:])
    norm = row_of(sums, 0)
    curve = row_of(sums, 1) + 2.0 * energy
    if first:
        return field, norm, curve, norm / curve, None
    turn = norm / scalars_in[0:1]
    bend = curve + turn * (2.0 * row_of(sums, 2) + turn * scalars_in[1:2])
    return field, norm, bend, norm / bend, turn


def column_sum(value):
    return jnp.sum(value, axis=0, keepdims=True)


def leaf_apply(vector, kernel, tall):
    low = vector.astype(BF)
    return dot(kernel, low) + ridge_weight * vector, dot(tall, low).astype(BF)


def close_leaves(mix, gathered, sums, near, payload):
    packed = jnp.concatenate(gathered, axis=0)
    below = LEAVES * RANK
    payload[:RANK] = dot(mix[below:], packed).astype(BF)
    felt = dot(mix[:below], packed)
    energy = column_sum(packed.astype(F32) * felt)
    near[...] = felt
    payload[RANK:] = pack_sums(sums + stack_rows(jnp.zeros_like(energy), energy))


def begin_kernel(residual, direction, kernel, tall, mix, base, near, payload):
    sums = None
    gathered = []
    for i in range(LEAVES):
        rows = slice(i * ROWS, (i + 1) * ROWS)
        vector = direction[rows]
        out, local = leaf_apply(vector, kernel[i], tall[i])
        base[rows] = out
        here = residual[rows]
        part = stack_rows(column_sum(here * here), column_sum(vector * out))
        sums = part if i == 0 else sums + part
        gathered.append(local)
    close_leaves(mix, gathered, sums, near, payload)


def leaf_fields(paths, near, field):
    every = (near[...] + dot(paths[...], field)).astype(BF)
    return [every[i * RANK : (i + 1) * RANK] for i in range(LEAVES)]


def turn_kernel(first, own, got, down, field_in, scalars_in, *rest):
    basis, paths, base_in, near_in = rest[:4]
    rest = rest[4:]
    if first:
        residual, image, kernel, tall, mix = rest[:5]
        residual_out, image_out, base, near, payload, scalars = rest[5:]
    else:
        residual, direction, image, kernel, tall, mix = rest[:6]
        residual_out, direction_out, image_out, base, near, payload, scalars = rest[6:]
    field, norm, bend, size, beta = finish_sweep(own, got, down, field_in, scalars_in, first)
    scalars[...] = stack_rows(norm, bend, size)
    fields = leaf_fields(paths, near_in, field)
    sums = None
    gathered = []
    for i in range(LEAVES):
        rows = slice(i * ROWS, (i + 1) * ROWS)
        pushed = base_in[rows] + dot(basis[i], fields[i])
        here = residual[rows]
        if not first:
            pushed = pushed + beta * image[rows]
            direction_out[rows] = here + beta * direction[rows]
        here = here - size * pushed
        residual_out[rows] = here
        image_out[rows] = pushed
        out, local = leaf_apply(here, kernel[i], tall[i])
        base[rows] = out
        part = stack_rows(column_sum(here * here), column_sum(here * out), column_sum(here * pushed))
        sums = part if i == 0 else sums + part
        gathered.append(local)
    close_leaves(mix, gathered, sums, near, payload)


def end_kernel(
    own,
    got,
    down,
    field_in,
    scalars_in,
    basis,
    paths,
    base_in,
    near_in,
    residual,
    direction,
    image,
    solved,
    residual_out,
    residual_kept,
    direction_out,
    solved_out,
    scalars,
    sums_out,
):
    field, norm, bend, size, beta = finish_sweep(own, got, down, field_in, scalars_in, False)
    scalars[...] = stack_rows(norm, bend, size)
    fields = leaf_fields(paths, near_in, field)
    sums = None
    for i in range(LEAVES):
        rows = slice(i * ROWS, (i + 1) * ROWS)
        pushed = base_in[rows] + dot(basis[i], fields[i])
        pushed = pushed + beta * image[rows]
        here = residual[rows]
        step = here + beta * direction[rows]
        direction_out[rows] = step
        solved_out[rows] = solved[rows] + size * step
        here = here - size * pushed
        residual_out[rows] = here
        residual_kept[rows] = here
        part = column_sum(here * here)
        sums = part if i == 0 else sums + part
    sums_out[...] = jnp.broadcast_to(sums, sums_out.shape)


def last_kernel(parts, residual, direction, scalars, out):
    beta = column_sum(parts[...]) / scalars[0:1]
    out[...] = residual[...] + beta * direction[...]


vector_shape = jax.ShapeDtypeStruct((LEAVES * ROWS, COLS), F32)
near_shape = jax.ShapeDtypeStruct((LEAVES * RANK, COLS), F32)
payload_shape = jax.ShapeDtypeStruct((PAYLOAD, COLS), BF)
field_shape = jax.ShapeDtypeStruct((RANK, COLS), F32)
small_shape = jax.ShapeDtypeStruct((8, COLS), F32)


def begin(residual, direction, kernels, tall, mix):
    return call(
        begin_kernel,
        "begin",
        (residual, direction, kernels, tall, mix),
        [vector_shape, near_shape, payload_shape],
    )


def turn(first, sweep, scalars, leaves, residual, direction, image, apply):
    vectors = (residual, image) if first else (residual, direction, image)
    results = call(
        functools.partial(turn_kernel, first),
        "turn",
        (*sweep, scalars, *leaves, *vectors, *apply),
        [vector_shape] * (len(vectors) + 1) + [near_shape, payload_shape, small_shape],
    )
    if first:
        return results[0], direction, *results[1:]
    return results


def end(sweep, scalars, leaves, residual, direction, image, solved, count):
    return call(
        end_kernel,
        "end",
        (*sweep, scalars, *leaves, residual, direction, image, solved),
        [vector_shape] * 4 + [small_shape, jax.ShapeDtypeStruct((count, COLS), F32)],
    )


def per_device(
    count,
    points,
    tree_order,
    leaf_basis,
    local_transfer,
    local_coupling,
    device_transfer,
    device_coupling,
    solution,
    residual,
    direction,
):
    routes = partners(count)
    kernels = make_kernels(points, tree_order)
    tall, mix, paths, *steps = compose(
        leaf_basis, local_transfer, local_coupling, device_transfer, kernels
    )
    others = [lax.ppermute(block, "leaf", route) for block, route in zip(steps, routes)]
    apply = (kernels, tall, mix)
    base, near, payload = begin(residual, direction, *apply)
    down = descend(local_transfer, device_transfer, device_coupling)
    image = direction
    scalars = jnp.ones((8, COLS), F32)
    for step in range(ITERATIONS):
        field = None
        for level in range(LEVELS - 1):
            got = lax.ppermute(payload, "leaf", routes[level])
            payload, field = climb(
                level, payload, got, steps[level], others[level], down, field
            )
        got = lax.ppermute(payload, "leaf", routes[LEVELS - 1])
        sweep = (payload, got, down, field)
        leaves = (leaf_basis, paths, base, near)
        if step + 1 < ITERATIONS:
            residual, direction, image, base, near, payload, scalars = turn(
                step == 0, sweep, scalars, leaves, residual, direction, image, apply
            )
            solution = solution + scalars[2:3] * direction
        else:
            residual, kept, direction, solution, scalars, sums = end(
                sweep, scalars, leaves, residual, direction, image, solution, count // 2
            )
    chip = sums + lax.ppermute(sums[0:1], "leaf", routes[0])
    same_core = [list(range(core, count, 2)) for core in range(2)]
    parts = lax.all_to_all(chip, "leaf", 0, 0, axis_index_groups=same_core, tiled=True)
    direction = call(last_kernel, "last", (parts, kept, direction, scalars), [vector_shape])[0]
    return (solution, residual, direction)


def solution(mesh):
    placed = (
        P(None, "leaf"),
        P("leaf", None),
        P("leaf", None, None),
        P("leaf", None, None),
        P("leaf", None, None),
        P("leaf", None, None, None),
        P("leaf", None, None, None),
        P("leaf", None),
        P("leaf", None),
        P("leaf", None),
    )
    return jax.shard_map(
        functools.partial(per_device, mesh.shape["leaf"]),
        mesh=mesh,
        in_specs=placed,
        out_specs=(P("leaf", None), P("leaf", None), P("leaf", None)),
        check_vma=False,
    )
```
